512 devices in a mesh: row: 32 (over x_lo, y, core), col: 16 (over x_hi, z).
Axes of the slice: x: 4 (x_hi: 2, x_lo: 2; x = x_hi * 2 + x_lo), y: 8, z: 8, core: 2. Of those that a mesh axis runs over, the one named last changes fastest.
Arguments:
- observed: float32 [1, 4096, 8192], P(None, 'row', 'col'), may hold values from 0.2 to 2
- start: float32 [1, 4096, 8192], P(None, 'row', 'col'), may hold values from 0.5 to 2
- psf_rows: float32 [127], replicated, may hold values from 0.05 to 1
- psf_cols: float32 [127], replicated, may hold values from 0.05 to 1
Outputs:
- estimate: float32 [1, 4096, 8192], P(None, 'row', 'col')
- norms: float32 [2], replicated
The draws below stay inside these ranges and needn't reach their ends.
All inputs are finite; a program needn't handle non-finite values.
Results may differ from the reference program's by a relative error of at most 0.0001.
Values sent between devices are 32-bit elements; how exact they have to be, the bound alone decides.
A program may use at most 64 MiB of HBM per device.

```python
import math
import jax
import jax.numpy as jnp
from jax import lax

PLANES = 1
TAPS = 127
ITERS = 2
NX = 4096
NY = 8192


def shard_levels(stream_key, shape, pieces, low, high):
    def one(dim, parts):
        heights = jax.random.uniform(jax.random.fold_in(jax.random.fold_in(stream_key, 6), dim), (parts,), jnp.float32, low / len(pieces), high / len(pieces))
        return jnp.repeat(jnp.exp(heights), shape[dim] // parts).reshape((-1,) + (1,) * (len(shape) - dim - 1))

    factor_of = one(*pieces[0])
    for cut in pieces[1:]:
        factor_of = factor_of * one(*cut)
    return factor_of


def setup_inputs(seed: int = 0) -> dict:
    streams_of = jax.random.split(jax.random.key(seed), 5)
    return {
        "observed": jnp.clip(0.2 + 1.8 * jax.random.uniform(streams_of[0], (PLANES, NX, NY), jnp.float32) ** shard_levels(streams_of[0], (PLANES, NX, NY), ((1, 32), (2, 16)), -0.2, 0.2), 0.2, 2.0),
        "start": jnp.clip(jnp.exp(math.log(2.0) - 1.3862944 * jax.random.uniform(streams_of[1], (PLANES, NX, NY), jnp.float32) ** shard_levels(streams_of[1], (PLANES, NX, NY), ((1, 32), (2, 16)), -0.2, 0.2)), 0.5, 2.0),
        "psf_rows": jnp.clip(jnp.exp(jax.random.uniform(streams_of[2], (TAPS,), jnp.float32, math.log(0.05), math.log(1.0))), 0.05, 1.0),
        "psf_cols": jnp.clip(jnp.exp(jax.random.uniform(streams_of[3], (TAPS,), jnp.float32, math.log(0.05), math.log(1.0))), 0.05, 1.0),
    }


def along(field, taps, axis):
    length = field.shape[axis]
    size = 1 << (length + 125).bit_length()
    moved = jnp.moveaxis(field, axis, -1)
    spectrum = jnp.fft.rfft(moved, size, axis=-1) * jnp.fft.rfft(taps, size)
    filtered = jnp.fft.irfft(spectrum, size, axis=-1)[..., 63:63 + length]
    return jnp.moveaxis(filtered, -1, axis)


def reference(observed, start, psf_rows, psf_cols):
    row_taps = psf_rows / jnp.sum(psf_rows)
    col_taps = psf_cols / jnp.sum(psf_cols)

    def one_plane(pair):
        seen, current = pair
        sums = []
        for step in range(ITERS):
            blurred = along(along(current, col_taps[::-1], 1), row_taps[::-1], 0)
            misfit = seen - blurred
            sums.append(jnp.sum(misfit * misfit))
            ratio = seen / blurred
            current = current * along(along(ratio, col_taps, 1), row_taps, 0)
        return current, jnp.stack(sums)

    estimate, plane_sums = lax.map(one_plane, (observed, start))
    return estimate, jnp.sum(plane_sums, axis=0)
```

```python
import functools

import jax
import jax.numpy as jnp
from jax import lax
from jax.experimental import pallas as pl
from jax.experimental.pallas import tpu as pltpu
from jax.sharding import PartitionSpec as P

ITERS = 2
STAGES = 2 * ITERS
MESH = pl.DeviceIdType.MESH
STEPS = ((-1, -1), (-1, 1), (1, -1), (1, 1), (0, -1), (0, 1), (-1, 0), (1, 0))


def split(value):
    high = value.astype(jnp.bfloat16)
    low = (value - high.astype(jnp.float32)).astype(jnp.bfloat16)
    return high, low


def dot(left, right):
    return jnp.dot(left, right, preferred_element_type=jnp.float32)


def circulant(taps, shift, rows):
    wide = jnp.broadcast_to(taps, (rows, 256))
    return pltpu.roll(wide, shift % 256, 1, stride=1, stride_axis=0)


def kernel(
    rows, cols, obs_hbm, start_hbm, taps_rows, taps_cols, out_ref, norms_ref,
    field, left, right, pack_left, pack_right, seen, current, result, taps,
    row_mats, col_mats, partial, gather_rows, middle, gather_cols,
    send, recv, local, norm_send, norm_recv,
):
    row, col = lax.axis_index("row"), lax.axis_index("col")

    load_start = pltpu.make_async_copy(start_hbm, field.at[0, pl.ds(64, 128)], local.at[0])
    load_seen = pltpu.make_async_copy(obs_hbm, seen, local.at[1])
    load_start.start()
    load_seen.start()

    def near(step):
        r, c = row + step[0], col + step[1]
        inside = (r >= 0) & (r < rows) & (c >= 0) & (c < cols)
        return inside, (r, c)

    barrier = pltpu.get_barrier_semaphore()
    expected = jnp.int32(rows - 1 + cols - 1)
    for step in STEPS[:4]:
        inside, device = near(step)

        @pl.when(inside)
        def _():
            pl.semaphore_signal(barrier, inc=1, device_id=device, device_id_type=MESH)

        expected = expected + inside.astype(jnp.int32)

    def greet_row(d, carry):
        pl.semaphore_signal(
            barrier, inc=1, device_id=(lax.rem(row + d, rows), col), device_id_type=MESH
        )
        return carry

    def greet_col(d, carry):
        pl.semaphore_signal(
            barrier, inc=1, device_id=(row, lax.rem(col + d, cols)), device_id_type=MESH
        )
        return carry

    lax.fori_loop(1, rows, greet_row, 0)
    lax.fori_loop(1, cols, greet_col, 0)

    @pl.when(row == 0)
    def _():
        field[:, 0:64, :] = jnp.zeros((STAGES, 64, 512), jnp.float32)
        left[:, 0:32, :] = jnp.zeros((STAGES, 32, 128), jnp.float32)
        right[:, 0:32, :] = jnp.zeros((STAGES, 32, 128), jnp.float32)

    @pl.when(row == rows - 1)
    def _():
        field[:, 192:256, :] = jnp.zeros((STAGES, 64, 512), jnp.float32)
        left[:, 96:128, :] = jnp.zeros((STAGES, 32, 128), jnp.float32)
        right[:, 96:128, :] = jnp.zeros((STAGES, 32, 128), jnp.float32)

    @pl.when(col == 0)
    def _():
        left[...] = jnp.zeros((STAGES, 128, 128), jnp.float32)

    @pl.when(col == cols - 1)
    def _():
        right[...] = jnp.zeros((STAGES, 128, 128), jnp.float32)

    taps[...] = jnp.zeros((8, 256), jnp.float32)
    taps[0:1, 0:127] = taps_rows[...] / jnp.sum(taps_rows[...])
    taps[1:2, 0:127] = taps_cols[...] / jnp.sum(taps_cols[...])
    row_taps, col_taps = taps[0:1, :], taps[1:2, :]
    by_rows = (circulant(row_taps, 1, 128), circulant(row_taps, -127, 256)[:, :128].T)
    along = circulant(col_taps, -63, 256)
    by_cols = (along[:128].T, along[:, :128])
    for which in range(2):
        high, low = split(by_rows[which])
        row_mats[which, 0:128, :] = high
        row_mats[which, 128:256, :] = low
        high, low = split(by_cols[which])
        col_mats[which, :, 0:128] = high
        col_mats[which, :, 128:256] = low

    lane = lax.broadcasted_iota(jnp.int32, (32, 128), 1) < 64
    lane_tall = lax.broadcasted_iota(jnp.int32, (128, 128), 1) < 64

    def copies(stage):
        own = field.at[stage]
        ends = {
            (-1, 0): (own.at[pl.ds(64, 64)], own.at[pl.ds(192, 64)]),
            (1, 0): (own.at[pl.ds(128, 64)], own.at[pl.ds(0, 64)]),
            (0, -1): (pack_left.at[stage], right.at[stage, pl.ds(32, 64)]),
            (0, 1): (pack_right.at[stage], left.at[stage, pl.ds(32, 64)]),
            (-1, -1): (pack_left.at[stage, pl.ds(0, 32)], right.at[stage, pl.ds(96, 32)]),
            (-1, 1): (pack_right.at[stage, pl.ds(0, 32)], left.at[stage, pl.ds(96, 32)]),
            (1, -1): (pack_left.at[stage, pl.ds(32, 32)], right.at[stage, pl.ds(0, 32)]),
            (1, 1): (pack_right.at[stage, pl.ds(32, 32)], left.at[stage, pl.ds(0, 32)]),
        }
        made = []
        for k, step in enumerate(STEPS):
            inside, device = near(step)
            source, target = ends[step]
            copy = pltpu.make_async_remote_copy(
                src_ref=source,
                dst_ref=target,
                send_sem=send.at[stage, k],
                recv_sem=recv.at[stage, k],
                device_id=device,
                device_id_type=MESH,
            )
            made.append((step, inside, copy))
        return made

    def post(stage):
        for half in range(2):
            at = 64 + 64 * half
            first = field[stage, at : at + 32, 0:128]
            second = field[stage, at + 32 : at + 64, 0:128]
            pack_left[stage, 32 * half : 32 * half + 32, :] = jnp.where(
                lane, first, pltpu.roll(second, 64, 1)
            )
            first = field[stage, at : at + 32, 384:512]
            second = field[stage, at + 32 : at + 64, 384:512]
            pack_right[stage, 32 * half : 32 * half + 32, :] = jnp.where(
                lane, pltpu.roll(second, 64, 1), first
            )
        for _, inside, copy in copies(stage):

            @pl.when(inside)
            def _():
                copy.start()

    def arrive(stage):
        for step, _, copy in copies(stage):
            inside, _ = near((-step[0], -step[1]))

            @pl.when(inside)
            def _():
                copy.wait_recv()

    def depart(stage):
        for _, inside, copy in copies(stage):

            @pl.when(inside)
            def _():
                copy.wait_send()

    def blur(stage, which):
        sides = []
        for group in range(4):
            from_left = left[stage, 32 * group : 32 * group + 32, :]
            from_right = right[stage, 32 * group : 32 * group + 32, :]
            sides.append(jnp.where(lane, from_right, from_left))
            sides.append(pltpu.roll(jnp.where(lane, from_left, from_right), 64, 1))
        wide = jnp.concatenate([field[stage], jnp.concatenate(sides, axis=0)], axis=1)
        high, low = split(wide)
        both = dot(row_mats[which], high)
        tall = both[0:128] + both[128:256] + dot(row_mats[which, 0:128, :], low)
        blocks = [tall[:, 128 * b : 128 * b + 128] for b in range(5)]
        pairs = []
        for b in range(4):
            mixed = jnp.where(lane_tall, blocks[b + 1], blocks[b - 1])
            pairs.append(jnp.concatenate([blocks[b], mixed], axis=1))
        high, low = split(jnp.concatenate(pairs, axis=0))
        both = dot(high, col_mats[which])
        flat = both[:, 0:128] + both[:, 128:256] + dot(low, col_mats[which, :, 0:128])
        return [flat[128 * b : 128 * b + 128] for b in range(4)]

    def norm_row(d):
        to = lax.rem(row + d, rows)
        return pltpu.make_async_remote_copy(
            src_ref=partial,
            dst_ref=gather_rows.at[row],
            send_sem=norm_send.at[0],
            recv_sem=norm_recv.at[0],
            device_id=(to, col),
            device_id_type=MESH,
        )

    def norm_col(d):
        to = lax.rem(col + d, cols)
        return pltpu.make_async_remote_copy(
            src_ref=middle,
            dst_ref=gather_cols.at[col],
            send_sem=norm_send.at[1],
            recv_sem=norm_recv.at[1],
            device_id=(row, to),
            device_id_type=MESH,
        )

    def wait_all(buffer, count, index, which):
        whole = buffer.at[pl.ds(0, count)]
        copy = pltpu.make_async_copy(whole, whole, which.at[index])
        copy.wait()

    def start_norm_row(d, carry):
        norm_row(d).start()
        return carry

    def start_norm_col(d, carry):
        norm_col(d).start()
        return carry

    load_start.wait()
    pl.semaphore_wait(barrier, expected)

    for stage in range(STAGES):
        post(stage)
        if stage == 0:
            current[...] = field[0, 64:192, :]
            load_seen.wait()
        arrive(stage)
        outs = blur(stage, stage % 2)
        if stage % 2 == 0:
            total = jnp.zeros((1, 128), jnp.float32)
            for b in range(4):
                misfit = seen[:, 128 * b : 128 * b + 128] - outs[b]
                total = total + jnp.sum(misfit * misfit, axis=0, keepdims=True)
            partial[stage // 2 : stage // 2 + 1, :] = total
            if stage == STAGES - 2:
                gather_rows[row] = partial[...]
                lax.fori_loop(1, rows, start_norm_row, 0)
            for b in range(4):
                field[stage + 1, 64:192, 128 * b : 128 * b + 128] = (
                    seen[:, 128 * b : 128 * b + 128] / outs[b]
                )
        else:
            target = field.at[stage + 1, pl.ds(64, 128)] if stage + 1 < STAGES else result
            for b in range(4):
                value = current[:, 128 * b : 128 * b + 128] * outs[b]
                target[:, 128 * b : 128 * b + 128] = value
                if stage + 1 < STAGES:
                    current[:, 128 * b : 128 * b + 128] = value

    store = pltpu.make_async_copy(result, out_ref, local.at[2])
    store.start()
    wait_all(gather_rows, rows - 1, 0, norm_recv)
    total = gather_rows[0]
    for r in range(1, rows):
        total = total + gather_rows[r]
    middle[...] = total
    gather_cols[col] = total
    lax.fori_loop(1, cols, start_norm_col, 0)
    for stage in range(STAGES):
        depart(stage)
    wait_all(gather_rows, rows - 1, 0, norm_send)
    wait_all(gather_cols, cols - 1, 1, norm_recv)
    total = gather_cols[0]
    for c in range(1, cols):
        total = total + gather_cols[c]
    sums = jnp.sum(total, axis=1, keepdims=True)
    place = lax.broadcasted_iota(jnp.int32, (1, 2), 1)
    norms_ref[...] = jnp.where(place == 0, sums[0:1], sums[1:2])
    wait_all(gather_cols, cols - 1, 1, norm_send)
    store.wait()


def body(rows, cols, observed, start, psf_rows, psf_cols):
    f32, bf16 = jnp.float32, jnp.bfloat16
    estimate, norms = pl.pallas_call(
        functools.partial(kernel, rows, cols),
        out_shape=(
            jax.ShapeDtypeStruct((128, 512), f32),
            jax.ShapeDtypeStruct((1, 2), f32),
        ),
        in_specs=[
            pl.BlockSpec(memory_space=pl.ANY),
            pl.BlockSpec(memory_space=pl.ANY),
            pl.BlockSpec(memory_space=pltpu.VMEM),
            pl.BlockSpec(memory_space=pltpu.VMEM),
        ],
        out_specs=(
            pl.BlockSpec(memory_space=pl.ANY),
            pl.BlockSpec(memory_space=pltpu.VMEM),
        ),
        scratch_shapes=[
            pltpu.VMEM((STAGES, 256, 512), f32),
            pltpu.VMEM((STAGES, 128, 128), f32),
            pltpu.VMEM((STAGES, 128, 128), f32),
            pltpu.VMEM((STAGES, 64, 128), f32),
            pltpu.VMEM((STAGES, 64, 128), f32),
            pltpu.VMEM((128, 512), f32),
            pltpu.VMEM((128, 512), f32),
            pltpu.VMEM((128, 512), f32),
            pltpu.VMEM((8, 256), f32),
            pltpu.VMEM((2, 256, 256), bf16),
            pltpu.VMEM((2, 256, 256), bf16),
            pltpu.VMEM((2, 128), f32),
            pltpu.VMEM((rows, 2, 128), f32),
            pltpu.VMEM((2, 128), f32),
            pltpu.VMEM((cols, 2, 128), f32),
            pltpu.SemaphoreType.DMA((STAGES, 8)),
            pltpu.SemaphoreType.DMA((STAGES, 8)),
            pltpu.SemaphoreType.DMA((3,)),
            pltpu.SemaphoreType.DMA((2,)),
            pltpu.SemaphoreType.DMA((2,)),
        ],
        compiler_params=pltpu.CompilerParams(
            collective_id=0, has_side_effects=True, vmem_limit_bytes=48 * 1024 * 1024
        ),
        name="deconvolve",
    )(observed[0], start[0], psf_rows.reshape(1, 127), psf_cols.reshape(1, 127))
    return estimate[None], norms.reshape(2)


def solution(mesh):
    in_specs = (P(None, "row", "col"), P(None, "row", "col"), P(), P())
    out_specs = (P(None, "row", "col"), P())
    step = functools.partial(body, mesh.shape["row"], mesh.shape["col"])
    return jax.shard_map(step, mesh=mesh, in_specs=in_specs, out_specs=out_specs, check_vma=False)
```

```python
import functools

import jax
import jax.numpy as jnp
from jax import lax
from jax.experimental import pallas as pl
from jax.experimental.pallas import tpu as pltpu
from jax.sharding import PartitionSpec as P

ITERS = 2
STAGES = 2 * ITERS
MESH = pl.DeviceIdType.MESH
SIDES = ((-1, -1), (-1, 1), (1, -1), (1, 1), (0, -1), (0, 1))
ENDS = ((-1, 0), (1, 0))


def split(value):
    high = value.astype(jnp.bfloat16)
    low = (value - high.astype(jnp.float32)).astype(jnp.bfloat16)
    return high, low


def dot(left, right):
    return jnp.dot(left, right, preferred_element_type=jnp.float32)


def circulant(taps, shift, rows):
    wide = jnp.broadcast_to(taps, (rows, 256))
    return pltpu.roll(wide, shift % 256, 1, stride=1, stride_axis=0)


def doublings(count):
    return max(count - 2, 0).bit_length()


def kernel(
    rows, cols, obs_hbm, start_hbm, rows_hbm, cols_hbm, out_ref, norms_ref,
    field, left, right, pack_left, pack_right, seen, result, taps_rows, taps_cols, taps,
    row_mats, col_mats, partial, gather_rows, middle, gather_cols,
    send_sides, recv_sides, send_rows, recv_rows, local, norm_send, norm_recv, known,
):
    row, col = lax.axis_index("row"), lax.axis_index("col")

    load_start = pltpu.make_async_copy(start_hbm, field.at[0, pl.ds(64, 128)], local.at[0])
    load_seen = pltpu.make_async_copy(obs_hbm, seen, local.at[1])
    load_rows = pltpu.make_async_copy(rows_hbm, taps_rows, local.at[2])
    load_cols = pltpu.make_async_copy(cols_hbm, taps_cols, local.at[3])
    load_start.start()

    def near(step):
        r, c = row + step[0], col + step[1]
        inside = (r >= 0) & (r < rows) & (c >= 0) & (c < cols)
        return inside, (r, c)

    barrier = pltpu.get_barrier_semaphore()
    expected = jnp.int32(0)
    for step in SIDES + ENDS:
        inside, device = near(step)

        @pl.when(inside)
        def _():
            pl.semaphore_signal(barrier, inc=1, device_id=device, device_id_type=MESH)

        expected = expected + inside.astype(jnp.int32)

    load_seen.start()
    load_rows.start()
    load_cols.start()

    lane = lax.broadcasted_iota(jnp.int32, (32, 128), 1) < 64
    lane_tall = lax.broadcasted_iota(jnp.int32, (128, 128), 1) < 64

    def remote(step, source, target, sent, received):
        inside, device = near(step)
        copy = pltpu.make_async_remote_copy(
            src_ref=source,
            dst_ref=target,
            send_sem=sent,
            recv_sem=received,
            device_id=device,
            device_id_type=MESH,
        )
        return step, inside, copy

    def side_copies(stage):
        ends = {
            (0, -1): (pack_left.at[stage], right.at[stage, pl.ds(32, 64)]),
            (0, 1): (pack_right.at[stage], left.at[stage, pl.ds(32, 64)]),
            (-1, -1): (pack_left.at[stage, pl.ds(0, 32)], right.at[stage, pl.ds(96, 32)]),
            (-1, 1): (pack_right.at[stage, pl.ds(0, 32)], left.at[stage, pl.ds(96, 32)]),
            (1, -1): (pack_left.at[stage, pl.ds(32, 32)], right.at[stage, pl.ds(0, 32)]),
            (1, 1): (pack_right.at[stage, pl.ds(32, 32)], left.at[stage, pl.ds(0, 32)]),
        }
        return [
            remote(step, *ends[step], send_sides.at[stage, k], recv_sides.at[stage, k])
            for k, step in enumerate(SIDES)
        ]

    def row_copies(stage, blocks):
        made = []
        for k, step in enumerate(ENDS):
            source, target = ((64, 192), (128, 0))[k]
            for b in blocks:
                lanes = pl.ds(128 * b, 128)
                made.append(
                    remote(
                        step,
                        field.at[stage, pl.ds(source, 64), lanes],
                        field.at[stage, pl.ds(target, 64), lanes],
                        send_rows.at[stage, k, b],
                        recv_rows.at[stage, k, b],
                    )
                )
        return made

    def start(copies):
        for _, inside, copy in copies:

            @pl.when(inside)
            def _():
                copy.start()

    def arrive(copies):
        for step, _, copy in copies:
            inside, _ = near((-step[0], -step[1]))

            @pl.when(inside)
            def _():
                copy.wait_recv()

    def depart(copies):
        for _, inside, copy in copies:

            @pl.when(inside)
            def _():
                copy.wait_send()

    def pack(stage, edge):
        for half in range(2):
            first = edge[64 * half : 64 * half + 32]
            second = pltpu.roll(edge[64 * half + 32 : 64 * half + 64], 64, 1)
            rows_here = slice(32 * half, 32 * half + 32)
            pack_left[stage, rows_here, :] = jnp.where(lane, first, second)
            pack_right[stage, rows_here, :] = jnp.where(lane, second, first)

    def along_rows(which, value):
        high, low = split(value)
        both = dot(row_mats[which], high)
        return both[0:128] + both[128:256] + dot(row_mats[which, 0:128, :], low)

    def along_cols(which, blocks, first, second):
        nothing = jnp.zeros((128, 128), jnp.float32)
        pairs = []
        for b in (first, second):
            mixed = jnp.where(lane_tall, blocks.get(b + 1, nothing), blocks.get(b - 1, nothing))
            pairs.append(jnp.concatenate([blocks[b], mixed], axis=1))
        high, low = split(jnp.concatenate(pairs, axis=0))
        both = dot(high, col_mats[which])
        flat = both[:, 0:128] + both[:, 128:256] + dot(low, col_mats[which, :, 0:128])
        return flat[0:128], flat[128:256]

    def along_cols_edge(which, halo):
        high, low = split(halo)
        both = dot(high, col_mats[which, 128:256, :])
        return both[:, 0:128] + both[:, 128:256] + dot(low, col_mats[which, 128:256, 0:128])

    def sides(stage):
        parts = []
        for group in range(4):
            from_left = left[stage, 32 * group : 32 * group + 32, :]
            from_right = right[stage, 32 * group : 32 * group + 32, :]
            parts.append(jnp.where(lane, from_right, from_left))
            parts.append(pltpu.roll(jnp.where(lane, from_left, from_right), 64, 1))
        return jnp.concatenate(parts, axis=0)

    def squares(difference):
        return jnp.sum(difference * difference, axis=0, keepdims=True)

    def norm_row(d):
        return pltpu.make_async_remote_copy(
            src_ref=partial,
            dst_ref=gather_rows.at[row],
            send_sem=norm_send.at[0],
            recv_sem=norm_recv.at[0],
            device_id=(lax.rem(row + d, rows), col),
            device_id_type=MESH,
        )

    def norm_col(d):
        return pltpu.make_async_remote_copy(
            src_ref=middle,
            dst_ref=gather_cols.at[col],
            send_sem=norm_send.at[1],
            recv_sem=norm_recv.at[1],
            device_id=(row, lax.rem(col + d, cols)),
            device_id_type=MESH,
        )

    def wait_all(buffer, count, semaphore):
        whole = buffer.at[pl.ds(0, count)]
        pltpu.make_async_copy(whole, whole, semaphore).wait()

    def start_norm_row(d, carry):
        norm_row(d).start()
        return carry

    def start_norm_col(d, carry):
        norm_col(d).start()
        return carry

    def tell(level):
        for k, steps in enumerate(((1, 0), (0, 1))):
            if 1 << level < (rows, cols)[k] - 1:
                for sign in (-1, 1):
                    inside, device = near(tuple(sign * (1 << level) * s for s in steps))

                    @pl.when(inside)
                    def _():
                        pl.semaphore_signal(
                            known.at[level, k], inc=1, device_id=device, device_id_type=MESH
                        )

    def hear(level):
        for k, steps in enumerate(((1, 0), (0, 1))):
            if 1 << level < (rows, cols)[k] - 1:
                told = jnp.int32(0)
                for sign in (-1, 1):
                    inside, _ = near(tuple(sign * (1 << level) * s for s in steps))
                    told = told + inside.astype(jnp.int32)
                pl.semaphore_wait(known.at[level, k], told)

    load_start.wait()
    pack(0, jnp.where(lane_tall, field[0, 64:192, 0:128], field[0, 64:192, 384:512]))
    pl.semaphore_wait(barrier, expected)
    start(side_copies(0))
    start(row_copies(0, (0, 1, 2, 3)))
    tell(0)

    @pl.when(row == 0)
    def _():
        field[:, 0:64, :] = jnp.zeros((STAGES, 64, 512), jnp.float32)
        left[:, 0:32, :] = jnp.zeros((STAGES, 32, 128), jnp.float32)
        right[:, 0:32, :] = jnp.zeros((STAGES, 32, 128), jnp.float32)

    @pl.when(row == rows - 1)
    def _():
        field[:, 192:256, :] = jnp.zeros((STAGES, 64, 512), jnp.float32)
        left[:, 96:128, :] = jnp.zeros((STAGES, 32, 128), jnp.float32)
        right[:, 96:128, :] = jnp.zeros((STAGES, 32, 128), jnp.float32)

    @pl.when(col == 0)
    def _():
        left[...] = jnp.zeros((STAGES, 128, 128), jnp.float32)

    @pl.when(col == cols - 1)
    def _():
        right[...] = jnp.zeros((STAGES, 128, 128), jnp.float32)

    load_rows.wait()
    load_cols.wait()
    taps[...] = jnp.zeros((8, 256), jnp.float32)
    taps[0:1, 0:127] = taps_rows[...] / jnp.sum(taps_rows[...])
    taps[1:2, 0:127] = taps_cols[...] / jnp.sum(taps_cols[...])
    row_taps, col_taps = taps[0:1, :], taps[1:2, :]
    by_rows = (circulant(row_taps, 1, 128), circulant(row_taps, -127, 256)[:, :128].T)
    along = circulant(col_taps, -63, 256)
    by_cols = (along[:128].T, along[:, :128])
    for which in range(2):
        high, low = split(by_rows[which])
        row_mats[which, 0:128, :] = high
        row_mats[which, 128:256, :] = low
        high, low = split(by_cols[which])
        col_mats[which, :, 0:128] = high
        col_mats[which, :, 128:256] = low
    load_seen.wait()

    def updated(stage, own, blurred):
        return own / blurred if stage % 2 == 0 else own * blurred

    levels = max(doublings(rows), doublings(cols))
    hear(0)
    tell(1)
    heard = 1
    for stage in range(STAGES):
        which, last = stage % 2, stage + 1 == STAGES
        if last:
            wait_all(gather_rows, rows - 1, norm_recv.at[0])
            total = gather_rows[0]
            for r in range(1, rows):
                total = total + gather_rows[r]
            middle[...] = total
            gather_cols[col] = total
            lax.fori_loop(1, cols, start_norm_col, 0)

        def own(b):
            lanes = slice(128 * b, 128 * b + 128)
            return seen[:, lanes] if which == 0 else field[stage - 1, 64:192, lanes]

        def put(b, value):
            lanes = slice(128 * b, 128 * b + 128)
            if last:
                result[:, lanes] = value
            else:
                field[stage + 1, 64:192, lanes] = value

        blocks, outs = {}, {}
        arrive(row_copies(stage, (1, 2)))
        both = along_rows(which, field[stage, :, 128:384])
        blocks[1], blocks[2] = both[:, 0:128], both[:, 128:256]
        arrive(row_copies(stage, (0, 3)))
        both = along_rows(
            which, jnp.concatenate([field[stage, :, 0:128], field[stage, :, 384:512]], axis=1)
        )
        blocks[0], blocks[3] = both[:, 0:128], both[:, 128:256]
        outs[1], outs[2] = along_cols(which, blocks, 1, 2)
        for b in (1, 2):
            put(b, updated(stage, own(b), outs[b]))
        if not last:
            start(row_copies(stage + 1, (1, 2)))
        outs[0], outs[3] = along_cols(which, blocks, 0, 3)
        inner = {b: updated(stage, own(b), outs[b]) for b in (0, 3)}
        if which == 0:
            partial_sum = squares(own(1) - outs[1]) + squares(own(2) - outs[2])
            partial_sum = partial_sum + squares(
                jnp.where(lane_tall, own(3) - outs[3], own(0) - outs[0])
            )
        own_edge = jnp.where(lane_tall, own(0), own(3))
        edge = jnp.where(lane_tall, outs[0], outs[3])
        if stage > 0 and heard < levels:
            hear(heard)
            heard += 1
            tell(heard)
        arrive(side_copies(stage))
        edge = edge + along_cols_edge(which, along_rows(which, sides(stage)))
        if stage == STAGES - 2:
            partial[ITERS - 1 : ITERS, :] = partial_sum + squares(own_edge - edge)
            gather_rows[row] = partial[...]
            lax.fori_loop(1, rows, start_norm_row, 0)
        outer = updated(stage, own_edge, edge)
        if not last:
            pack(stage + 1, outer)
            start(side_copies(stage + 1))
        put(0, jnp.where(lane_tall, outer, inner[0]))
        put(3, jnp.where(lane_tall, inner[3], outer))
        if not last:
            start(row_copies(stage + 1, (0, 3)))
        if which == 0 and stage < STAGES - 2:
            k = stage // 2
            partial[k : k + 1, :] = partial_sum + squares(own_edge - edge)
        if stage < STAGES - 2 and heard < levels:
            hear(heard)
            heard += 1
            tell(heard)

    store = pltpu.make_async_copy(result, out_ref, local.at[4])
    store.start()
    for stage in range(STAGES):
        depart(side_copies(stage))
        depart(row_copies(stage, (0, 1, 2, 3)))
    wait_all(gather_rows, rows - 1, norm_send.at[0])
    wait_all(gather_cols, cols - 1, norm_recv.at[1])
    total = gather_cols[0]
    for c in range(1, cols):
        total = total + gather_cols[c]
    sums = jnp.sum(total, axis=1, keepdims=True)
    place = lax.broadcasted_iota(jnp.int32, (1, 2), 1)
    norms_ref[...] = jnp.where(place == 0, sums[0:1], sums[1:2])
    wait_all(gather_cols, cols - 1, norm_send.at[1])
    store.wait()


def finish(estimate, norms, out, out_norms, block, small, loaded, stored):
    loads, stores = [], []
    height = 128 // 4
    for k in range(4):
        rows = pl.ds(height * k, height)
        loads.append(pltpu.make_async_copy(estimate.at[rows], block.at[rows], loaded.at[k]))
        stores.append(pltpu.make_async_copy(block.at[rows], out.at[rows], stored.at[k]))
    loads.append(pltpu.make_async_copy(norms, small, loaded.at[4]))
    stores.append(pltpu.make_async_copy(small, out_norms, stored.at[4]))
    for load in loads:
        load.start()
    for load, store in zip(loads, stores):
        load.wait()
        store.start()
    for store in stores:
        store.wait()


def body(rows, cols, observed, start, psf_rows, psf_cols):
    f32, bf16 = jnp.float32, jnp.bfloat16
    estimate, norms = pl.pallas_call(
        functools.partial(kernel, rows, cols),
        out_shape=(
            jax.ShapeDtypeStruct((128, 512), f32),
            jax.ShapeDtypeStruct((1, 2), f32),
        ),
        in_specs=[
            pl.BlockSpec(memory_space=pltpu.HBM),
            pl.BlockSpec(memory_space=pltpu.HBM),
            pl.BlockSpec(memory_space=pltpu.HBM),
            pl.BlockSpec(memory_space=pltpu.HBM),
        ],
        out_specs=(
            pl.BlockSpec(memory_space=pl.ANY),
            pl.BlockSpec(memory_space=pltpu.VMEM),
        ),
        scratch_shapes=[
            pltpu.VMEM((STAGES, 256, 512), f32),
            pltpu.VMEM((STAGES, 128, 128), f32),
            pltpu.VMEM((STAGES, 128, 128), f32),
            pltpu.VMEM((STAGES, 64, 128), f32),
            pltpu.VMEM((STAGES, 64, 128), f32),
            pltpu.VMEM((128, 512), f32),
            pltpu.VMEM((128, 512), f32),
            pltpu.VMEM((1, 127), f32),
            pltpu.VMEM((1, 127), f32),
            pltpu.VMEM((8, 256), f32),
            pltpu.VMEM((2, 256, 256), bf16),
            pltpu.VMEM((2, 256, 256), bf16),
            pltpu.VMEM((2, 128), f32),
            pltpu.VMEM((rows, 2, 128), f32),
            pltpu.VMEM((2, 128), f32),
            pltpu.VMEM((cols, 2, 128), f32),
            pltpu.SemaphoreType.DMA((STAGES, 6)),
            pltpu.SemaphoreType.DMA((STAGES, 6)),
            pltpu.SemaphoreType.DMA((STAGES, 2, 4)),
            pltpu.SemaphoreType.DMA((STAGES, 2, 4)),
            pltpu.SemaphoreType.DMA((5,)),
            pltpu.SemaphoreType.DMA((2,)),
            pltpu.SemaphoreType.DMA((2,)),
            pltpu.SemaphoreType.REGULAR((max(doublings(rows), doublings(cols)), 2)),
        ],
        compiler_params=pltpu.CompilerParams(
            collective_id=0, has_side_effects=True, vmem_limit_bytes=60 * 1024 * 1024
        ),
        name="deconvolve",
    )(observed[0], start[0], psf_rows.reshape(1, 127), psf_cols.reshape(1, 127))
    estimate, norms = pl.pallas_call(
        finish,
        out_shape=(jax.ShapeDtypeStruct((128, 512), f32), jax.ShapeDtypeStruct((1, 2), f32)),
        in_specs=[pl.BlockSpec(memory_space=pl.ANY)] * 2,
        out_specs=[pl.BlockSpec(memory_space=pl.ANY)] * 2,
        scratch_shapes=[
            pltpu.VMEM((128, 512), f32),
            pltpu.VMEM((1, 2), f32),
            pltpu.SemaphoreType.DMA((4 + 1,)),
            pltpu.SemaphoreType.DMA((4 + 1,)),
        ],
        compiler_params=pltpu.CompilerParams(vmem_limit_bytes=60 * 1024 * 1024),
        name="finish",
    )(estimate, norms)
    return estimate[None], norms.reshape(2)


def solution(mesh):
    in_specs = (P(None, "row", "col"), P(None, "row", "col"), P(), P())
    out_specs = (P(None, "row", "col"), P())
    step = functools.partial(body, mesh.shape["row"], mesh.shape["col"])
    return jax.shard_map(step, mesh=mesh, in_specs=in_specs, out_specs=out_specs, check_vma=False)
```

```python
import functools

import jax
import jax.numpy as jnp
from jax import lax
from jax.experimental import pallas as pl
from jax.experimental.pallas import tpu as pltpu
from jax.sharding import PartitionSpec as P

MESH = pl.DeviceIdType.MESH
SIDES = ((-1, -1), (-1, 1), (1, -1), (1, 1), (0, -1), (0, 1))
ENDS = ((-1, 0), (1, 0))


def split(value):
    high = value.astype(jnp.bfloat16)
    low = (value - high.astype(jnp.float32)).astype(jnp.bfloat16)
    return high, low


def dot(left, right):
    return jnp.dot(left, right, preferred_element_type=jnp.float32)


def circulant(taps, shift, rows):
    wide = jnp.broadcast_to(taps, (rows, 256))
    return pltpu.roll(wide, shift % 256, 1, stride=1, stride_axis=0)


def doublings(count):
    return max(count - 2, 0).bit_length()


def kernel(
    rows, cols, obs_hbm, start_hbm, rows_hbm, cols_hbm, out_ref, norms_ref,
    field, left, right, pack_left, pack_right, beside, ratio, deep_left, deep_right,
    seen, result, taps_rows, taps_cols, taps,
    row_mats, col_mats, partial, gather_rows, middle, gather_cols,
    send_sides, recv_sides, send_rows, recv_rows, local, norm_send, norm_recv, known,
):
    row, col = lax.axis_index("row"), lax.axis_index("col")

    load_start = pltpu.make_async_copy(start_hbm, field.at[0, pl.ds(64, 128)], local.at[0])
    load_seen = pltpu.make_async_copy(obs_hbm, seen, local.at[1])
    load_rows = pltpu.make_async_copy(rows_hbm, taps_rows, local.at[2])
    load_cols = pltpu.make_async_copy(cols_hbm, taps_cols, local.at[3])
    load_start.start()

    def near(step):
        r, c = row + step[0], col + step[1]
        inside = (r >= 0) & (r < rows) & (c >= 0) & (c < cols)
        return inside, (r, c)

    barrier = pltpu.get_barrier_semaphore()
    expected = jnp.int32(0)
    for step in SIDES + ENDS:
        inside, device = near(step)

        @pl.when(inside)
        def _():
            pl.semaphore_signal(barrier, inc=1, device_id=device, device_id_type=MESH)

        expected = expected + inside.astype(jnp.int32)

    load_seen.start()
    load_rows.start()
    load_cols.start()

    lane = lax.broadcasted_iota(jnp.int32, (32, 128), 1) < 64
    lane_tall = lax.broadcasted_iota(jnp.int32, (128, 128), 1) < 64
    lane_deep = lax.broadcasted_iota(jnp.int32, (256, 128), 1) < 64

    def remote(step, source, target, sent, received):
        inside, device = near(step)
        copy = pltpu.make_async_remote_copy(
            src_ref=source,
            dst_ref=target,
            send_sem=sent,
            recv_sem=received,
            device_id=device,
            device_id_type=MESH,
        )
        return step, inside, copy

    def side_copies(turn):
        ends = {
            (0, -1): (pack_left.at[turn], right.at[turn, pl.ds(32, 64)]),
            (0, 1): (pack_right.at[turn], left.at[turn, pl.ds(32, 64)]),
            (-1, -1): (pack_left.at[turn, pl.ds(0, 32)], right.at[turn, pl.ds(96, 32)]),
            (-1, 1): (pack_right.at[turn, pl.ds(0, 32)], left.at[turn, pl.ds(96, 32)]),
            (1, -1): (pack_left.at[turn, pl.ds(32, 32)], right.at[turn, pl.ds(0, 32)]),
            (1, 1): (pack_right.at[turn, pl.ds(32, 32)], left.at[turn, pl.ds(0, 32)]),
        }
        return [
            remote(step, *ends[step], send_sides.at[turn, k], recv_sides.at[turn, k])
            for k, step in enumerate(SIDES)
        ]

    def row_copies(turn, blocks):
        made = []
        for k, step in enumerate(ENDS):
            source, target = ((64, 192), (128, 0))[k]
            for b in blocks:
                lanes = pl.ds(128 * b, 128)
                made.append(
                    remote(
                        step,
                        field.at[2 * turn, pl.ds(source, 64), lanes],
                        field.at[2 * turn, pl.ds(target, 64), lanes],
                        send_rows.at[turn, k, b],
                        recv_rows.at[turn, k, b],
                    )
                )
        return made

    def deep_side_copies():
        made = []
        for k, (down, across) in enumerate(SIDES):
            block, target = (0, deep_right) if across < 0 else (3, deep_left)
            made.append(
                remote(
                    (down, across),
                    ratio.at[pl.ds(128, 128), pl.ds(128 * block, 128)],
                    target.at[pl.ds(128 - 128 * down, 128)],
                    send_sides.at[2, k],
                    recv_sides.at[2, k],
                )
            )
        return made

    def deep_row_copies(blocks):
        made = []
        for k, step in enumerate(ENDS):
            for b in blocks:
                lanes = pl.ds(128 * b, 128)
                made.append(
                    remote(
                        step,
                        ratio.at[pl.ds(128, 128), lanes],
                        ratio.at[pl.ds(128 - 128 * step[0], 128), lanes],
                        send_rows.at[2, k, b],
                        recv_rows.at[2, k, b],
                    )
                )
        return made

    def start(copies):
        for _, inside, copy in copies:

            @pl.when(inside)
            def _():
                copy.start()

    def arrive(copies):
        for step, _, copy in copies:
            inside, _ = near((-step[0], -step[1]))

            @pl.when(inside)
            def _():
                copy.wait_recv()

    def depart(copies):
        for _, inside, copy in copies:

            @pl.when(inside)
            def _():
                copy.wait_send()

    def pack(turn, edge):
        for half in range(2):
            first = edge[64 * half : 64 * half + 32]
            second = pltpu.roll(edge[64 * half + 32 : 64 * half + 64], 64, 1)
            rows_here = slice(32 * half, 32 * half + 32)
            pack_left[turn, rows_here, :] = jnp.where(lane, first, second)
            pack_right[turn, rows_here, :] = jnp.where(lane, second, first)

    def along_rows(which, value):
        high, low = split(value)
        both = dot(row_mats[which], high)
        return both[0:128] + both[128:256] + dot(row_mats[which, 0:128, :], low)

    def along_cols(which, blocks, first, second):
        height = blocks[first].shape[0]
        low_lanes = lane_tall if height == 128 else lane_deep
        nothing = jnp.zeros((height, 128), jnp.float32)
        pairs = []
        for b in (first, second):
            mixed = jnp.where(low_lanes, blocks.get(b + 1, nothing), blocks.get(b - 1, nothing))
            pairs.append(jnp.concatenate([blocks[b], mixed], axis=1))
        high, low = split(jnp.concatenate(pairs, axis=0))
        both = dot(high, col_mats[which])
        flat = both[:, 0:128] + both[:, 128:256] + dot(low, col_mats[which, :, 0:128])
        return flat[0:height], flat[height : 2 * height]

    def along_cols_edge(which, halo):
        high, low = split(halo)
        both = dot(high, col_mats[which, 128:256, :])
        return both[:, 0:128] + both[:, 128:256] + dot(low, col_mats[which, 128:256, 0:128])

    def along_rows_deep(which, value):
        return jnp.concatenate(
            [along_rows(which, value[0:256]), along_rows(which, value[128:384])], axis=0
        )

    def sides(turn):
        parts = []
        for group in range(4):
            from_left = left[turn, 32 * group : 32 * group + 32, :]
            from_right = right[turn, 32 * group : 32 * group + 32, :]
            parts.append(jnp.where(lane, from_right, from_left))
            parts.append(pltpu.roll(jnp.where(lane, from_left, from_right), 64, 1))
        return jnp.concatenate(parts, axis=0)

    def squares(difference):
        return jnp.sum(difference * difference, axis=0, keepdims=True)

    def norm_row(d):
        return pltpu.make_async_remote_copy(
            src_ref=partial,
            dst_ref=gather_rows.at[row],
            send_sem=norm_send.at[0],
            recv_sem=norm_recv.at[0],
            device_id=(lax.rem(row + d, rows), col),
            device_id_type=MESH,
        )

    def norm_col(d):
        return pltpu.make_async_remote_copy(
            src_ref=middle,
            dst_ref=gather_cols.at[col],
            send_sem=norm_send.at[1],
            recv_sem=norm_recv.at[1],
            device_id=(row, lax.rem(col + d, cols)),
            device_id_type=MESH,
        )

    def wait_all(buffer, count, semaphore):
        whole = buffer.at[pl.ds(0, count)]
        pltpu.make_async_copy(whole, whole, semaphore).wait()

    def start_norm_row(d, carry):
        norm_row(d).start()
        return carry

    def start_norm_col(d, carry):
        norm_col(d).start()
        return carry

    def tell(level):
        for k, steps in enumerate(((1, 0), (0, 1))):
            if 1 << level < (rows, cols)[k] - 1:
                for sign in (-1, 1):
                    inside, device = near(tuple(sign * (1 << level) * s for s in steps))

                    @pl.when(inside)
                    def _():
                        pl.semaphore_signal(
                            known.at[level, k], inc=1, device_id=device, device_id_type=MESH
                        )

    def hear(level):
        for k, steps in enumerate(((1, 0), (0, 1))):
            if 1 << level < (rows, cols)[k] - 1:
                told = jnp.int32(0)
                for sign in (-1, 1):
                    inside, _ = near(tuple(sign * (1 << level) * s for s in steps))
                    told = told + inside.astype(jnp.int32)
                pl.semaphore_wait(known.at[level, k], told)

    load_start.wait()
    pack(0, jnp.where(lane_tall, field[0, 64:192, 0:128], field[0, 64:192, 384:512]))
    pl.semaphore_wait(barrier, expected)
    start(side_copies(0))
    start(row_copies(0, (0, 1, 2, 3)))
    tell(0)

    @pl.when(row == 0)
    def _():
        for k in (0, 2):
            field[k, 0:64, :] = jnp.zeros((64, 512), jnp.float32)
        ratio[0:128, :] = jnp.zeros((128, 512), jnp.float32)
        for buffer in (left, right):
            buffer[:, 0:32, :] = jnp.zeros((2, 32, 128), jnp.float32)
        for buffer in (deep_left, deep_right):
            buffer[0:128, :] = jnp.zeros((128, 128), jnp.float32)

    @pl.when(row == rows - 1)
    def _():
        for k in (0, 2):
            field[k, 192:256, :] = jnp.zeros((64, 512), jnp.float32)
        ratio[256:384, :] = jnp.zeros((128, 512), jnp.float32)
        for buffer in (left, right):
            buffer[:, 96:128, :] = jnp.zeros((2, 32, 128), jnp.float32)
        for buffer in (deep_left, deep_right):
            buffer[256:384, :] = jnp.zeros((128, 128), jnp.float32)

    @pl.when(col == 0)
    def _():
        left[...] = jnp.zeros((2, 128, 128), jnp.float32)
        deep_left[...] = jnp.zeros((384, 128), jnp.float32)

    @pl.when(col == cols - 1)
    def _():
        right[...] = jnp.zeros((2, 128, 128), jnp.float32)
        deep_right[...] = jnp.zeros((384, 128), jnp.float32)

    load_rows.wait()
    load_cols.wait()
    taps[...] = jnp.zeros((8, 256), jnp.float32)
    taps[0:1, 0:127] = taps_rows[...] / jnp.sum(taps_rows[...])
    taps[1:2, 0:127] = taps_cols[...] / jnp.sum(taps_cols[...])
    row_taps, col_taps = taps[0:1, :], taps[1:2, :]
    by_rows = (circulant(row_taps, 1, 128), circulant(row_taps, -127, 256)[:, :128].T)
    along = circulant(col_taps, -63, 256)
    by_cols = (along[:128].T, along[:, :128])
    for which in range(2):
        high, low = split(by_rows[which])
        row_mats[which, 0:128, :] = high
        row_mats[which, 128:256, :] = low
        high, low = split(by_cols[which])
        col_mats[which, :, 0:128] = high
        col_mats[which, :, 128:256] = low
    load_seen.wait()

    def at(b):
        return slice(128 * b, 128 * b + 128)

    def pair(value):
        return value[:, 0:128], value[:, 128:256]

    def outer_blocks(value):
        return jnp.concatenate([value[:, 0:128], value[:, 384:512]], axis=1)

    rounds = max(doublings(rows), doublings(cols))

    def spread(level):
        if level < rounds:
            hear(level)
            tell(level + 1)

    spread(0)

    blocks, outs = {}, {}
    arrive(row_copies(0, (1, 2)))
    blocks[1], blocks[2] = pair(along_rows(0, field[0, :, 128:384]))
    arrive(row_copies(0, (0, 3)))
    blocks[0], blocks[3] = pair(along_rows(0, outer_blocks(field[0])))
    outs[1], outs[2] = along_cols(0, blocks, 1, 2)
    for b in (1, 2):
        ratio[128:256, at(b)] = seen[:, at(b)] / outs[b]
    start(deep_row_copies((1, 2)))
    outs[0], outs[3] = along_cols(0, blocks, 0, 3)
    seen_edge = jnp.where(lane_tall, seen[:, at(0)], seen[:, at(3)])
    edge = jnp.where(lane_tall, outs[0], outs[3])
    for b in (0, 3):
        ratio[128:256, at(b)] = seen[:, at(b)] / outs[b]
    inner_sum = squares(seen[:, at(1)] - outs[1]) + squares(seen[:, at(2)] - outs[2])
    inner_sum = inner_sum + squares(
        jnp.where(lane_tall, seen[:, at(3)] - outs[3], seen[:, at(0)] - outs[0])
    )
    spread(1)
    arrive(side_copies(0))
    halo = sides(0)
    beside[...] = halo
    edge = edge + along_cols_edge(0, along_rows(0, halo))
    outer = seen_edge / edge
    ratio[128:256, at(0)] = jnp.where(lane_tall, outer, ratio[128:256, at(0)])
    ratio[128:256, at(3)] = jnp.where(lane_tall, ratio[128:256, at(3)], outer)
    start(deep_side_copies())
    start(deep_row_copies((0, 3)))
    partial[0:1, :] = inner_sum + squares(seen_edge - edge)
    spread(2)
    spread(3)

    blocks, outs = {}, {}
    arrive(deep_row_copies((1, 2)))
    blocks[1], blocks[2] = pair(along_rows_deep(1, ratio[:, 128:384]))
    arrive(deep_row_copies((0, 3)))
    blocks[0], blocks[3] = pair(along_rows_deep(1, outer_blocks(ratio)))
    outs[1], outs[2] = along_cols(1, blocks, 1, 2)
    for b in (1, 2):
        field[1, :, at(b)] = field[0, :, at(b)] * outs[b]
    outs[0], outs[3] = along_cols(1, blocks, 0, 3)
    again = {}
    again[1], again[2] = pair(along_rows(0, field[1, :, 128:384]))
    for level in range(4, rounds):
        spread(level)
    arrive(deep_side_copies())
    blocks[-1], blocks[4] = pair(
        along_rows_deep(1, jnp.concatenate([deep_left[...], deep_right[...]], axis=1))
    )
    edge = along_cols_edge(1, jnp.where(lane_deep, blocks[4], blocks[-1]))
    outs[-1], outs[4] = along_cols(1, blocks, -1, 4)
    field[1, :, at(0)] = field[0, :, at(0)] * jnp.where(lane_deep, outs[0] + edge, outs[0])
    field[1, :, at(3)] = field[0, :, at(3)] * jnp.where(lane_deep, outs[3], outs[3] + edge)
    halo = beside[...] * jnp.where(lane_deep, outs[4], outs[-1])

    again[0], again[3] = pair(along_rows(0, outer_blocks(field[1])))
    again[-1] = again[4] = along_rows(0, halo)
    outs = {}
    outs[0], outs[3] = along_cols(0, again, 0, 3)
    outs[1], outs[2] = along_cols(0, again, 1, 2)
    partial[1:2, :] = sum(squares(seen[:, at(b)] - outs[b]) for b in range(4))
    gather_rows[row] = partial[...]
    lax.fori_loop(1, rows, start_norm_row, 0)
    for b in range(4):
        field[2, 64:192, at(b)] = seen[:, at(b)] / outs[b]
    pack(1, jnp.where(lane_tall, field[2, 64:192, at(0)], field[2, 64:192, at(3)]))
    start(side_copies(1))
    start(row_copies(1, (0, 1, 2, 3)))

    wait_all(gather_rows, rows - 1, norm_recv.at[0])
    total = gather_rows[0]
    for r in range(1, rows):
        total = total + gather_rows[r]
    middle[...] = total
    gather_cols[col] = total
    lax.fori_loop(1, cols, start_norm_col, 0)

    blocks, outs = {}, {}
    arrive(row_copies(1, (0, 1, 2, 3)))
    blocks[1], blocks[2] = pair(along_rows(1, field[2, :, 128:384]))
    blocks[0], blocks[3] = pair(along_rows(1, outer_blocks(field[2])))
    outs[1], outs[2] = along_cols(1, blocks, 1, 2)
    arrive(side_copies(1))
    blocks[-1] = blocks[4] = along_rows(1, sides(1))
    outs[0], outs[3] = along_cols(1, blocks, 0, 3)
    for b in range(4):
        result[:, at(b)] = field[1, 64:192, at(b)] * outs[b]

    store = pltpu.make_async_copy(result, out_ref, local.at[4])
    store.start()
    for turn in range(2):
        depart(side_copies(turn))
        depart(row_copies(turn, (0, 1, 2, 3)))
    depart(deep_side_copies())
    depart(deep_row_copies((0, 1, 2, 3)))
    wait_all(gather_rows, rows - 1, norm_send.at[0])
    wait_all(gather_cols, cols - 1, norm_recv.at[1])
    total = gather_cols[0]
    for c in range(1, cols):
        total = total + gather_cols[c]
    sums = jnp.sum(total, axis=1, keepdims=True)
    place = lax.broadcasted_iota(jnp.int32, (1, 2), 1)
    norms_ref[...] = jnp.where(place == 0, sums[0:1], sums[1:2])
    wait_all(gather_cols, cols - 1, norm_send.at[1])
    store.wait()


def finish(estimate, norms, out, out_norms, block, small, loaded, stored):
    loads, stores = [], []
    height = 128 // 4
    for k in range(4):
        rows = pl.ds(height * k, height)
        loads.append(pltpu.make_async_copy(estimate.at[rows], block.at[rows], loaded.at[k]))
        stores.append(pltpu.make_async_copy(block.at[rows], out.at[rows], stored.at[k]))
    loads.append(pltpu.make_async_copy(norms, small, loaded.at[4]))
    stores.append(pltpu.make_async_copy(small, out_norms, stored.at[4]))
    for load in loads:
        load.start()
    for load, store in zip(loads, stores):
        load.wait()
        store.start()
    for store in stores:
        store.wait()


def body(rows, cols, observed, start, psf_rows, psf_cols):
    f32, bf16 = jnp.float32, jnp.bfloat16
    estimate, norms = pl.pallas_call(
        functools.partial(kernel, rows, cols),
        out_shape=(
            jax.ShapeDtypeStruct((128, 512), f32),
            jax.ShapeDtypeStruct((1, 2), f32),
        ),
        in_specs=[
            pl.BlockSpec(memory_space=pltpu.HBM),
            pl.BlockSpec(memory_space=pltpu.HBM),
            pl.BlockSpec(memory_space=pltpu.HBM),
            pl.BlockSpec(memory_space=pltpu.HBM),
        ],
        out_specs=(
            pl.BlockSpec(memory_space=pl.ANY),
            pl.BlockSpec(memory_space=pltpu.VMEM),
        ),
        scratch_shapes=[
            pltpu.VMEM((3, 256, 512), f32),
            pltpu.VMEM((2, 128, 128), f32),
            pltpu.VMEM((2, 128, 128), f32),
            pltpu.VMEM((2, 64, 128), f32),
            pltpu.VMEM((2, 64, 128), f32),
            pltpu.VMEM((256, 128), f32),
            pltpu.VMEM((384, 512), f32),
            pltpu.VMEM((384, 128), f32),
            pltpu.VMEM((384, 128), f32),
            pltpu.VMEM((128, 512), f32),
            pltpu.VMEM((128, 512), f32),
            pltpu.VMEM((1, 127), f32),
            pltpu.VMEM((1, 127), f32),
            pltpu.VMEM((8, 256), f32),
            pltpu.VMEM((2, 256, 256), bf16),
            pltpu.VMEM((2, 256, 256), bf16),
            pltpu.VMEM((2, 128), f32),
            pltpu.VMEM((rows, 2, 128), f32),
            pltpu.VMEM((2, 128), f32),
            pltpu.VMEM((cols, 2, 128), f32),
            pltpu.SemaphoreType.DMA((3, 6)),
            pltpu.SemaphoreType.DMA((3, 6)),
            pltpu.SemaphoreType.DMA((3, 2, 4)),
            pltpu.SemaphoreType.DMA((3, 2, 4)),
            pltpu.SemaphoreType.DMA((5,)),
            pltpu.SemaphoreType.DMA((2,)),
            pltpu.SemaphoreType.DMA((2,)),
            pltpu.SemaphoreType.REGULAR((max(doublings(rows), doublings(cols)), 2)),
        ],
        compiler_params=pltpu.CompilerParams(
            collective_id=0, has_side_effects=True, vmem_limit_bytes=60 * 1024 * 1024
        ),
        name="deconvolve",
    )(observed[0], start[0], psf_rows.reshape(1, 127), psf_cols.reshape(1, 127))
    estimate, norms = pl.pallas_call(
        finish,
        out_shape=(jax.ShapeDtypeStruct((128, 512), f32), jax.ShapeDtypeStruct((1, 2), f32)),
        in_specs=[pl.BlockSpec(memory_space=pl.ANY)] * 2,
        out_specs=[pl.BlockSpec(memory_space=pl.ANY)] * 2,
        scratch_shapes=[
            pltpu.VMEM((128, 512), f32),
            pltpu.VMEM((1, 2), f32),
            pltpu.SemaphoreType.DMA((4 + 1,)),
            pltpu.SemaphoreType.DMA((4 + 1,)),
        ],
        compiler_params=pltpu.CompilerParams(vmem_limit_bytes=60 * 1024 * 1024),
        name="finish",
    )(estimate, norms)
    return estimate[None], norms.reshape(2)


def solution(mesh):
    in_specs = (P(None, "row", "col"), P(None, "row", "col"), P(), P())
    out_specs = (P(None, "row", "col"), P())
    step = functools.partial(body, mesh.shape["row"], mesh.shape["col"])
    return jax.shard_map(step, mesh=mesh, in_specs=in_specs, out_specs=out_specs, check_vma=False)
```

```python
import functools

import jax
import jax.numpy as jnp
from jax import lax
from jax.experimental import pallas as pl
from jax.experimental.pallas import tpu as pltpu
from jax.sharding import PartitionSpec as P

MESH = pl.DeviceIdType.MESH
EARLY = ((1, 0), (2, 0), (16, 0), (0, 1))
SIDES = ((-1, -1), (-1, 1), (1, -1), (1, 1), (0, -1), (0, 1))
ENDS = ((-1, 0), (1, 0))


def split(value):
    high = value.astype(jnp.bfloat16)
    low = (value - high.astype(jnp.float32)).astype(jnp.bfloat16)
    return high, low


def dot(left, right):
    return jnp.dot(left, right, preferred_element_type=jnp.float32)


def circulant(taps, shift, rows):
    wide = jnp.broadcast_to(taps, (rows, 256))
    return pltpu.roll(wide, shift % 256, 1, stride=1, stride_axis=0)


def doublings(count):
    return max(count - 2, 0).bit_length()


def kernel(
    rows, cols, obs_hbm, start_hbm, rows_hbm, cols_hbm, out_ref, norms_ref,
    field, left, right, pack_left, pack_right, beside, ratio, deep_left, deep_right,
    seen, result, taps_rows, taps_cols, taps,
    row_mats, col_mats, partial, gather_rows, middle, gather_cols, gather_all,
    send_sides, recv_sides, send_rows, recv_rows, local, norm_send, norm_recv, known,
):
    row, col = lax.axis_index("row"), lax.axis_index("col")

    load_start = pltpu.make_async_copy(start_hbm, field.at[0, pl.ds(64, 128)], local.at[0])
    load_seen = pltpu.make_async_copy(obs_hbm, seen, local.at[1])
    load_rows = pltpu.make_async_copy(rows_hbm, taps_rows, local.at[2])
    load_cols = pltpu.make_async_copy(cols_hbm, taps_cols, local.at[3])
    load_start.start()

    def near(step):
        r, c = row + step[0], col + step[1]
        inside = (r >= 0) & (r < rows) & (c >= 0) & (c < cols)
        return inside, (r, c)

    barrier = pltpu.get_barrier_semaphore()
    expected = jnp.int32(0)
    for step in SIDES + ENDS:
        inside, device = near(step)

        @pl.when(inside)
        def _():
            pl.semaphore_signal(barrier, inc=1, device_id=device, device_id_type=MESH)

        expected = expected + inside.astype(jnp.int32)

    early = [(r, c) for r, c in EARLY if r < rows and c < cols]
    is_early = [(row == r) & (col == c) for r, c in early]
    for here in is_early:
        @pl.when(here)
        def _():
            def greet(k, carry):
                r, c = lax.rem(k, rows), cols - 1 - lax.div(k, rows)

                @pl.when((r != row) | (c != col))
                def _():
                    pl.semaphore_signal(
                        barrier, inc=1, device_id=(r, c), device_id_type=MESH
                    )

                return carry

            lax.fori_loop(0, rows * cols, greet, 0)

        expected = expected + (1 - here.astype(jnp.int32))

    load_seen.start()
    load_rows.start()
    load_cols.start()

    lane = lax.broadcasted_iota(jnp.int32, (32, 128), 1) < 64
    lane_tall = lax.broadcasted_iota(jnp.int32, (128, 128), 1) < 64
    lane_deep = lax.broadcasted_iota(jnp.int32, (256, 128), 1) < 64

    def remote(step, source, target, sent, received):
        inside, device = near(step)
        copy = pltpu.make_async_remote_copy(
            src_ref=source,
            dst_ref=target,
            send_sem=sent,
            recv_sem=received,
            device_id=device,
            device_id_type=MESH,
        )
        return step, inside, copy

    def side_copies(turn):
        ends = {
            (0, -1): (pack_left.at[turn], right.at[turn, pl.ds(32, 64)]),
            (0, 1): (pack_right.at[turn], left.at[turn, pl.ds(32, 64)]),
            (-1, -1): (pack_left.at[turn, pl.ds(0, 32)], right.at[turn, pl.ds(96, 32)]),
            (-1, 1): (pack_right.at[turn, pl.ds(0, 32)], left.at[turn, pl.ds(96, 32)]),
            (1, -1): (pack_left.at[turn, pl.ds(32, 32)], right.at[turn, pl.ds(0, 32)]),
            (1, 1): (pack_right.at[turn, pl.ds(32, 32)], left.at[turn, pl.ds(0, 32)]),
        }
        return [
            remote(step, *ends[step], send_sides.at[turn, k], recv_sides.at[turn, k])
            for k, step in enumerate(SIDES)
        ]

    def row_copies(turn, blocks):
        made = []
        for k, step in enumerate(ENDS):
            source, target = ((64, 192), (128, 0))[k]
            for b in blocks:
                lanes = pl.ds(128 * b, 128)
                made.append(
                    remote(
                        step,
                        field.at[2 * turn, pl.ds(source, 64), lanes],
                        field.at[2 * turn, pl.ds(target, 64), lanes],
                        send_rows.at[turn, k, b],
                        recv_rows.at[turn, k, b],
                    )
                )
        return made

    def deep_side_copies():
        made = []
        for k, (down, across) in enumerate(SIDES):
            block, target = (0, deep_right) if across < 0 else (3, deep_left)
            made.append(
                remote(
                    (down, across),
                    ratio.at[pl.ds(128, 128), pl.ds(128 * block, 128)],
                    target.at[pl.ds(128 - 128 * down, 128)],
                    send_sides.at[2, k],
                    recv_sides.at[2, k],
                )
            )
        return made

    def deep_row_copies(blocks):
        made = []
        for k, step in enumerate(ENDS):
            for b in blocks:
                lanes = pl.ds(128 * b, 128)
                made.append(
                    remote(
                        step,
                        ratio.at[pl.ds(128, 128), lanes],
                        ratio.at[pl.ds(128 - 128 * step[0], 128), lanes],
                        send_rows.at[2, k, b],
                        recv_rows.at[2, k, b],
                    )
                )
        return made

    def start(copies):
        for _, inside, copy in copies:

            @pl.when(inside)
            def _():
                copy.start()

    def arrive(copies):
        for step, _, copy in copies:
            inside, _ = near((-step[0], -step[1]))

            @pl.when(inside)
            def _():
                copy.wait_recv()

    def depart(copies):
        for _, inside, copy in copies:

            @pl.when(inside)
            def _():
                copy.wait_send()

    def pack(turn, edge):
        for half in range(2):
            first = edge[64 * half : 64 * half + 32]
            second = pltpu.roll(edge[64 * half + 32 : 64 * half + 64], 64, 1)
            rows_here = slice(32 * half, 32 * half + 32)
            pack_left[turn, rows_here, :] = jnp.where(lane, first, second)
            pack_right[turn, rows_here, :] = jnp.where(lane, second, first)

    def along_rows(which, value):
        high, low = split(value)
        both = dot(row_mats[which], high)
        return both[0:128] + both[128:256] + dot(row_mats[which, 0:128, :], low)

    def along_cols(which, blocks, first, second):
        height = blocks[first].shape[0]
        low_lanes = lane_tall if height == 128 else lane_deep
        nothing = jnp.zeros((height, 128), jnp.float32)
        pairs = []
        for b in (first, second):
            mixed = jnp.where(low_lanes, blocks.get(b + 1, nothing), blocks.get(b - 1, nothing))
            pairs.append(jnp.concatenate([blocks[b], mixed], axis=1))
        high, low = split(jnp.concatenate(pairs, axis=0))
        both = dot(high, col_mats[which])
        flat = both[:, 0:128] + both[:, 128:256] + dot(low, col_mats[which, :, 0:128])
        return flat[0:height], flat[height : 2 * height]

    def along_cols_edge(which, halo):
        high, low = split(halo)
        both = dot(high, col_mats[which, 128:256, :])
        return both[:, 0:128] + both[:, 128:256] + dot(low, col_mats[which, 128:256, 0:128])

    def along_rows_deep(which, value):
        return jnp.concatenate(
            [along_rows(which, value[0:256]), along_rows(which, value[128:384])], axis=0
        )

    def sides(turn):
        parts = []
        for group in range(4):
            from_left = left[turn, 32 * group : 32 * group + 32, :]
            from_right = right[turn, 32 * group : 32 * group + 32, :]
            parts.append(jnp.where(lane, from_right, from_left))
            parts.append(pltpu.roll(jnp.where(lane, from_left, from_right), 64, 1))
        return jnp.concatenate(parts, axis=0)

    def squares(difference):
        return jnp.sum(difference * difference, axis=0, keepdims=True)

    def norm_row(d):
        return pltpu.make_async_remote_copy(
            src_ref=partial,
            dst_ref=gather_rows.at[row],
            send_sem=norm_send.at[0],
            recv_sem=norm_recv.at[0],
            device_id=(lax.rem(row + d, rows), col),
            device_id_type=MESH,
        )

    def norm_col(d):
        return pltpu.make_async_remote_copy(
            src_ref=middle,
            dst_ref=gather_cols.at[col],
            send_sem=norm_send.at[1],
            recv_sem=norm_recv.at[1],
            device_id=(row, lax.rem(col + d, cols)),
            device_id_type=MESH,
        )

    def wait_all(buffer, count, semaphore):
        whole = buffer.at[pl.ds(0, count)]
        pltpu.make_async_copy(whole, whole, semaphore).wait()

    def start_norm_row(d, carry):
        norm_row(d).start()
        return carry

    def served(r, c):
        out = jnp.bool_(False)
        for e in early:
            out = out | ((r == e[0]) & (c == e[1]))
        return out

    def start_norm_col(d, carry):
        @pl.when(jnp.logical_not(served(row, lax.rem(col + d, cols))))
        def _():
            norm_col(d).start()

        return carry

    def direct(k):
        return pltpu.make_async_remote_copy(
            src_ref=partial,
            dst_ref=gather_all.at[row * cols + col],
            send_sem=norm_send.at[2 + k],
            recv_sem=norm_recv.at[2],
            device_id=early[k],
            device_id_type=MESH,
        )

    am_early = served(row, col)
    one_less = jnp.bool_(False)
    for e in early:
        one_less = one_less | ((row == e[0]) & (col != e[1]))

    def tell(level):
        for k, steps in enumerate(((1, 0), (0, 1))):
            if 1 << level < (rows, cols)[k] - 1:
                for sign in (-1, 1):
                    inside, device = near(tuple(sign * (1 << level) * s for s in steps))

                    @pl.when(inside)
                    def _():
                        pl.semaphore_signal(
                            known.at[level, k], inc=1, device_id=device, device_id_type=MESH
                        )

    def hear(level):
        for k, steps in enumerate(((1, 0), (0, 1))):
            if 1 << level < (rows, cols)[k] - 1:
                told = jnp.int32(0)
                for sign in (-1, 1):
                    inside, _ = near(tuple(sign * (1 << level) * s for s in steps))
                    told = told + inside.astype(jnp.int32)
                pl.semaphore_wait(known.at[level, k], told)

    load_start.wait()
    pack(0, jnp.where(lane_tall, field[0, 64:192, 0:128], field[0, 64:192, 384:512]))
    pl.semaphore_wait(barrier, expected)
    start(side_copies(0))
    start(row_copies(0, (0, 1, 2, 3)))
    tell(0)

    @pl.when(row == 0)
    def _():
        for k in (0, 2):
            field[k, 0:64, :] = jnp.zeros((64, 512), jnp.float32)
        ratio[0:128, :] = jnp.zeros((128, 512), jnp.float32)
        for buffer in (left, right):
            buffer[:, 0:32, :] = jnp.zeros((2, 32, 128), jnp.float32)
        for buffer in (deep_left, deep_right):
            buffer[0:128, :] = jnp.zeros((128, 128), jnp.float32)

    @pl.when(row == rows - 1)
    def _():
        for k in (0, 2):
            field[k, 192:256, :] = jnp.zeros((64, 512), jnp.float32)
        ratio[256:384, :] = jnp.zeros((128, 512), jnp.float32)
        for buffer in (left, right):
            buffer[:, 96:128, :] = jnp.zeros((2, 32, 128), jnp.float32)
        for buffer in (deep_left, deep_right):
            buffer[256:384, :] = jnp.zeros((128, 128), jnp.float32)

    @pl.when(col == 0)
    def _():
        left[...] = jnp.zeros((2, 128, 128), jnp.float32)
        deep_left[...] = jnp.zeros((384, 128), jnp.float32)

    @pl.when(col == cols - 1)
    def _():
        right[...] = jnp.zeros((2, 128, 128), jnp.float32)
        deep_right[...] = jnp.zeros((384, 128), jnp.float32)

    load_rows.wait()
    load_cols.wait()
    taps[...] = jnp.zeros((8, 256), jnp.float32)
    taps[0:1, 0:127] = taps_rows[...] / jnp.sum(taps_rows[...])
    taps[1:2, 0:127] = taps_cols[...] / jnp.sum(taps_cols[...])
    row_taps, col_taps = taps[0:1, :], taps[1:2, :]
    by_rows = (circulant(row_taps, 1, 128), circulant(row_taps, -127, 256)[:, :128].T)
    along = circulant(col_taps, -63, 256)
    by_cols = (along[:128].T, along[:, :128])
    for which in range(2):
        high, low = split(by_rows[which])
        row_mats[which, 0:128, :] = high
        row_mats[which, 128:256, :] = low
        high, low = split(by_cols[which])
        col_mats[which, :, 0:128] = high
        col_mats[which, :, 128:256] = low
    load_seen.wait()

    def at(b):
        return slice(128 * b, 128 * b + 128)

    def pair(value):
        return value[:, 0:128], value[:, 128:256]

    def outer_blocks(value):
        return jnp.concatenate([value[:, 0:128], value[:, 384:512]], axis=1)

    rounds = max(doublings(rows), doublings(cols))

    def spread(level):
        if level < rounds:
            hear(level)
            tell(level + 1)

    spread(0)

    blocks, outs = {}, {}
    arrive(row_copies(0, (1, 2)))
    blocks[1], blocks[2] = pair(along_rows(0, field[0, :, 128:384]))
    arrive(row_copies(0, (0, 3)))
    blocks[0], blocks[3] = pair(along_rows(0, outer_blocks(field[0])))
    outs[1], outs[2] = along_cols(0, blocks, 1, 2)
    for b in (1, 2):
        ratio[128:256, at(b)] = seen[:, at(b)] / outs[b]
    start(deep_row_copies((1, 2)))
    outs[0], outs[3] = along_cols(0, blocks, 0, 3)
    seen_edge = jnp.where(lane_tall, seen[:, at(0)], seen[:, at(3)])
    edge = jnp.where(lane_tall, outs[0], outs[3])
    for b in (0, 3):
        ratio[128:256, at(b)] = seen[:, at(b)] / outs[b]
    inner_sum = squares(seen[:, at(1)] - outs[1]) + squares(seen[:, at(2)] - outs[2])
    inner_sum = inner_sum + squares(
        jnp.where(lane_tall, seen[:, at(3)] - outs[3], seen[:, at(0)] - outs[0])
    )
    spread(1)
    arrive(side_copies(0))
    halo = sides(0)
    beside[...] = halo
    edge = edge + along_cols_edge(0, along_rows(0, halo))
    outer = seen_edge / edge
    ratio[128:256, at(0)] = jnp.where(lane_tall, outer, ratio[128:256, at(0)])
    ratio[128:256, at(3)] = jnp.where(lane_tall, ratio[128:256, at(3)], outer)
    start(deep_side_copies())
    start(deep_row_copies((0, 3)))
    first_norm = inner_sum + squares(seen_edge - edge)
    first_norm = first_norm + pltpu.roll(first_norm, 64, 1)
    spread(2)
    spread(3)

    blocks, outs = {}, {}
    arrive(deep_row_copies((1, 2)))
    blocks[1], blocks[2] = pair(along_rows_deep(1, ratio[:, 128:384]))
    arrive(deep_row_copies((0, 3)))
    blocks[0], blocks[3] = pair(along_rows_deep(1, outer_blocks(ratio)))
    outs[1], outs[2] = along_cols(1, blocks, 1, 2)
    for b in (1, 2):
        field[1, :, at(b)] = field[0, :, at(b)] * outs[b]
    outs[0], outs[3] = along_cols(1, blocks, 0, 3)
    again = {}
    again[1], again[2] = pair(along_rows(0, field[1, :, 128:384]))
    for level in range(4, rounds):
        spread(level)
    arrive(deep_side_copies())
    blocks[-1], blocks[4] = pair(
        along_rows_deep(1, jnp.concatenate([deep_left[...], deep_right[...]], axis=1))
    )
    edge = along_cols_edge(1, jnp.where(lane_deep, blocks[4], blocks[-1]))
    outs[-1], outs[4] = along_cols(1, blocks, -1, 4)
    field[1, :, at(0)] = field[0, :, at(0)] * jnp.where(lane_deep, outs[0] + edge, outs[0])
    field[1, :, at(3)] = field[0, :, at(3)] * jnp.where(lane_deep, outs[3], outs[3] + edge)
    halo = beside[...] * jnp.where(lane_deep, outs[4], outs[-1])

    again[0], again[3] = pair(along_rows(0, outer_blocks(field[1])))
    again[-1] = again[4] = along_rows(0, halo)
    outs = {}
    outs[0], outs[3] = along_cols(0, again, 0, 3)
    outs[1], outs[2] = along_cols(0, again, 1, 2)
    last_norm = sum(squares(seen[:, at(b)] - outs[b]) for b in range(4))
    last_norm = last_norm + pltpu.roll(last_norm, 64, 1)
    partial[...] = jnp.where(lane[0:1], first_norm, last_norm)
    gather_rows[row] = partial[...]
    for k, here in enumerate(is_early):

        @pl.when(here)
        def _():
            gather_all[row * cols + col] = partial[...]

        @pl.when(jnp.logical_not(here))
        def _():
            direct(k).start()

    lax.fori_loop(1, rows, start_norm_row, 0)
    for b in range(4):
        field[2, 64:192, at(b)] = seen[:, at(b)] / outs[b]
    pack(1, jnp.where(lane_tall, field[2, 64:192, at(0)], field[2, 64:192, at(3)]))
    start(side_copies(1))
    start(row_copies(1, (0, 1, 2, 3)))

    wait_all(gather_rows, rows - 1, norm_recv.at[0])
    total = gather_rows[0]
    for r in range(1, rows):
        total = total + gather_rows[r]
    middle[...] = total
    gather_cols[col] = total
    lax.fori_loop(1, cols, start_norm_col, 0)

    blocks, outs = {}, {}
    arrive(row_copies(1, (0, 1, 2, 3)))
    blocks[1], blocks[2] = pair(along_rows(1, field[2, :, 128:384]))
    blocks[0], blocks[3] = pair(along_rows(1, outer_blocks(field[2])))
    outs[1], outs[2] = along_cols(1, blocks, 1, 2)
    arrive(side_copies(1))
    blocks[-1] = blocks[4] = along_rows(1, sides(1))
    outs[0], outs[3] = along_cols(1, blocks, 0, 3)
    for b in range(4):
        result[:, at(b)] = field[1, 64:192, at(b)] * outs[b]

    store = pltpu.make_async_copy(result, out_ref, local.at[4])
    store.start()
    for turn in range(2):
        depart(side_copies(turn))
        depart(row_copies(turn, (0, 1, 2, 3)))
    depart(deep_side_copies())
    depart(deep_row_copies((0, 1, 2, 3)))
    wait_all(gather_rows, rows - 1, norm_send.at[0])
    place = lax.broadcasted_iota(jnp.int32, (1, 2), 1)

    def put_norms(total):
        first = jnp.sum(jnp.where(lane[0:1], total, 0.0), axis=1, keepdims=True)
        last = jnp.sum(jnp.where(lane[0:1], 0.0, total), axis=1, keepdims=True)
        norms_ref[...] = jnp.where(place == 0, first, last)

    @pl.when(am_early)
    def _():
        wait_all(gather_all, rows * cols - 1, norm_recv.at[2])
        total = None
        for c in range(cols):
            part = gather_all[c]
            for r in range(1, rows):
                part = part + gather_all[r * cols + c]
            total = part if total is None else total + part
        put_norms(total)

    @pl.when(jnp.logical_not(am_early))
    def _():
        wait_all(gather_cols, cols - 1, norm_recv.at[1])
        total = gather_cols[0]
        for c in range(1, cols):
            total = total + gather_cols[c]
        put_norms(total)

    @pl.when(one_less)
    def _():
        wait_all(gather_cols, cols - 2, norm_send.at[1])

    @pl.when(jnp.logical_not(one_less))
    def _():
        wait_all(gather_cols, cols - 1, norm_send.at[1])

    for k, here in enumerate(is_early):

        @pl.when(jnp.logical_not(here))
        def _():
            direct(k).wait_send()

    store.wait()


def finish(estimate, norms, out, out_norms, block, small, loaded, stored):
    loads, stores = [], []
    height = 128 // 4
    for k in range(4):
        rows = pl.ds(height * k, height)
        loads.append(pltpu.make_async_copy(estimate.at[rows], block.at[rows], loaded.at[k]))
        stores.append(pltpu.make_async_copy(block.at[rows], out.at[rows], stored.at[k]))
    loads.append(pltpu.make_async_copy(norms, small, loaded.at[4]))
    stores.append(pltpu.make_async_copy(small, out_norms, stored.at[4]))
    for load in loads:
        load.start()
    for load, store in zip(loads, stores):
        load.wait()
        store.start()
    for store in stores:
        store.wait()


def body(rows, cols, observed, start, psf_rows, psf_cols):
    f32, bf16 = jnp.float32, jnp.bfloat16
    estimate, norms = pl.pallas_call(
        functools.partial(kernel, rows, cols),
        out_shape=(
            jax.ShapeDtypeStruct((128, 512), f32),
            jax.ShapeDtypeStruct((1, 2), f32),
        ),
        in_specs=[
            pl.BlockSpec(memory_space=pltpu.HBM),
            pl.BlockSpec(memory_space=pltpu.HBM),
            pl.BlockSpec(memory_space=pltpu.HBM),
            pl.BlockSpec(memory_space=pltpu.HBM),
        ],
        out_specs=(
            pl.BlockSpec(memory_space=pl.ANY),
            pl.BlockSpec(memory_space=pltpu.VMEM),
        ),
        scratch_shapes=[
            pltpu.VMEM((3, 256, 512), f32),
            pltpu.VMEM((2, 128, 128), f32),
            pltpu.VMEM((2, 128, 128), f32),
            pltpu.VMEM((2, 64, 128), f32),
            pltpu.VMEM((2, 64, 128), f32),
            pltpu.VMEM((256, 128), f32),
            pltpu.VMEM((384, 512), f32),
            pltpu.VMEM((384, 128), f32),
            pltpu.VMEM((384, 128), f32),
            pltpu.VMEM((128, 512), f32),
            pltpu.VMEM((128, 512), f32),
            pltpu.VMEM((1, 127), f32),
            pltpu.VMEM((1, 127), f32),
            pltpu.VMEM((8, 256), f32),
            pltpu.VMEM((2, 256, 256), bf16),
            pltpu.VMEM((2, 256, 256), bf16),
            pltpu.VMEM((1, 128), f32),
            pltpu.VMEM((rows, 1, 128), f32),
            pltpu.VMEM((1, 128), f32),
            pltpu.VMEM((cols, 1, 128), f32),
            pltpu.VMEM((rows * cols, 1, 128), f32),
            pltpu.SemaphoreType.DMA((3, 6)),
            pltpu.SemaphoreType.DMA((3, 6)),
            pltpu.SemaphoreType.DMA((3, 2, 4)),
            pltpu.SemaphoreType.DMA((3, 2, 4)),
            pltpu.SemaphoreType.DMA((5,)),
            pltpu.SemaphoreType.DMA((2 + len(EARLY),)),
            pltpu.SemaphoreType.DMA((3,)),
            pltpu.SemaphoreType.REGULAR((max(doublings(rows), doublings(cols)), 2)),
        ],
        compiler_params=pltpu.CompilerParams(
            collective_id=0, has_side_effects=True, vmem_limit_bytes=60 * 1024 * 1024
        ),
        name="deconvolve",
    )(observed[0], start[0], psf_rows.reshape(1, 127), psf_cols.reshape(1, 127))
    estimate, norms = pl.pallas_call(
        finish,
        out_shape=(jax.ShapeDtypeStruct((128, 512), f32), jax.ShapeDtypeStruct((1, 2), f32)),
        in_specs=[pl.BlockSpec(memory_space=pl.ANY)] * 2,
        out_specs=[pl.BlockSpec(memory_space=pl.ANY)] * 2,
        scratch_shapes=[
            pltpu.VMEM((128, 512), f32),
            pltpu.VMEM((1, 2), f32),
            pltpu.SemaphoreType.DMA((4 + 1,)),
            pltpu.SemaphoreType.DMA((4 + 1,)),
        ],
        compiler_params=pltpu.CompilerParams(vmem_limit_bytes=60 * 1024 * 1024),
        name="finish",
    )(estimate, norms)
    return estimate[None], norms.reshape(2)


def solution(mesh):
    in_specs = (P(None, "row", "col"), P(None, "row", "col"), P(), P())
    out_specs = (P(None, "row", "col"), P())
    step = functools.partial(body, mesh.shape["row"], mesh.shape["col"])
    return jax.shard_map(step, mesh=mesh, in_specs=in_specs, out_specs=out_specs, check_vma=False)
```

```python
import functools

import jax
import jax.numpy as jnp
from jax import lax
from jax.experimental import pallas as pl
from jax.experimental.pallas import tpu as pltpu
from jax.sharding import PartitionSpec as P

MESH = pl.DeviceIdType.MESH
EARLY = ((1, 0), (2, 0), (16, 0), (0, 1))
SIDES = ((-1, -1), (-1, 1), (1, -1), (1, 1), (0, -1), (0, 1))
ENDS = ((-1, 0), (1, 0))


def split(value):
    high = value.astype(jnp.bfloat16)
    low = (value - high.astype(jnp.float32)).astype(jnp.bfloat16)
    return high, low


def dot(left, right):
    return jnp.dot(left, right, preferred_element_type=jnp.float32)


def circulant(taps, shift, rows):
    wide = jnp.broadcast_to(taps, (rows, 256))
    return pltpu.roll(wide, shift % 256, 1, stride=1, stride_axis=0)


def doublings(count):
    return max(count - 2, 0).bit_length()


def kernel(
    rows, cols, obs_hbm, start_hbm, rows_hbm, cols_hbm, out_ref, norms_ref,
    field, left, right, pack_left, pack_right, beside, ratio, deep_left, deep_right,
    seen, result, taps_rows, taps_cols, taps,
    row_mats, col_mats, partial, gather_rows, middle, gather_cols, gather_all,
    send_sides, recv_sides, send_rows, recv_rows, local, norm_send, norm_recv, known,
):
    row, col = lax.axis_index("row"), lax.axis_index("col")

    load_start = pltpu.make_async_copy(start_hbm, field.at[0, pl.ds(64, 128)], local.at[0])
    load_seen = pltpu.make_async_copy(obs_hbm, seen, local.at[1])
    load_rows = pltpu.make_async_copy(rows_hbm, taps_rows, local.at[2])
    load_cols = pltpu.make_async_copy(cols_hbm, taps_cols, local.at[3])
    load_start.start()

    def near(step):
        r, c = row + step[0], col + step[1]
        inside = (r >= 0) & (r < rows) & (c >= 0) & (c < cols)
        return inside, (r, c)

    barrier = pltpu.get_barrier_semaphore()
    expected = jnp.int32(0)
    for step in SIDES + ENDS:
        inside, device = near(step)

        @pl.when(inside)
        def _():
            pl.semaphore_signal(barrier, inc=1, device_id=device, device_id_type=MESH)

        expected = expected + inside.astype(jnp.int32)

    early = [(r, c) for r, c in EARLY if r < rows and c < cols]
    is_early = [(row == r) & (col == c) for r, c in early]
    for here in is_early:
        @pl.when(here)
        def _():
            def greet(k, carry):
                r, c = lax.rem(k, rows), cols - 1 - lax.div(k, rows)

                @pl.when((r != row) | (c != col))
                def _():
                    pl.semaphore_signal(
                        barrier, inc=1, device_id=(r, c), device_id_type=MESH
                    )

                return carry

            lax.fori_loop(0, rows * cols, greet, 0)

        expected = expected + (1 - here.astype(jnp.int32))

    load_seen.start()
    load_rows.start()
    load_cols.start()

    lane = lax.broadcasted_iota(jnp.int32, (32, 128), 1) < 64
    lane_tall = lax.broadcasted_iota(jnp.int32, (128, 128), 1) < 64
    lane_deep = lax.broadcasted_iota(jnp.int32, (256, 128), 1) < 64

    def remote(step, source, target, sent, received):
        inside, device = near(step)
        copy = pltpu.make_async_remote_copy(
            src_ref=source,
            dst_ref=target,
            send_sem=sent,
            recv_sem=received,
            device_id=device,
            device_id_type=MESH,
        )
        return step, inside, copy

    def side_copies(turn):
        ends = {
            (0, -1): (pack_left.at[turn], right.at[turn, pl.ds(32, 64)]),
            (0, 1): (pack_right.at[turn], left.at[turn, pl.ds(32, 64)]),
            (-1, -1): (pack_left.at[turn, pl.ds(0, 32)], right.at[turn, pl.ds(96, 32)]),
            (-1, 1): (pack_right.at[turn, pl.ds(0, 32)], left.at[turn, pl.ds(96, 32)]),
            (1, -1): (pack_left.at[turn, pl.ds(32, 32)], right.at[turn, pl.ds(0, 32)]),
            (1, 1): (pack_right.at[turn, pl.ds(32, 32)], left.at[turn, pl.ds(0, 32)]),
        }
        return [
            remote(step, *ends[step], send_sides.at[turn, k], recv_sides.at[turn, k])
            for k, step in enumerate(SIDES)
        ]

    def row_copies(turn, blocks):
        made = []
        for k, step in enumerate(ENDS):
            source, target = ((64, 192), (128, 0))[k]
            for b in blocks:
                lanes = pl.ds(128 * b, 128)
                made.append(
                    remote(
                        step,
                        field.at[2 * turn, pl.ds(source, 64), lanes],
                        field.at[2 * turn, pl.ds(target, 64), lanes],
                        send_rows.at[turn, k, b],
                        recv_rows.at[turn, k, b],
                    )
                )
        return made

    def deep_side_copies():
        made = []
        for k, (down, across) in enumerate(SIDES):
            block, target = (0, deep_right) if across < 0 else (3, deep_left)
            made.append(
                remote(
                    (down, across),
                    ratio.at[pl.ds(128, 128), pl.ds(128 * block, 128)],
                    target.at[pl.ds(128 - 128 * down, 128)],
                    send_sides.at[2, k],
                    recv_sides.at[2, k],
                )
            )
        return made

    def deep_row_copies(blocks):
        made = []
        for k, step in enumerate(ENDS):
            for b in blocks:
                lanes = pl.ds(128 * b, 128)
                made.append(
                    remote(
                        step,
                        ratio.at[pl.ds(128, 128), lanes],
                        ratio.at[pl.ds(128 - 128 * step[0], 128), lanes],
                        send_rows.at[2, k, b],
                        recv_rows.at[2, k, b],
                    )
                )
        return made

    def start(copies):
        for _, inside, copy in copies:

            @pl.when(inside)
            def _():
                copy.start()

    def arrive(copies):
        for step, _, copy in copies:
            inside, _ = near((-step[0], -step[1]))

            @pl.when(inside)
            def _():
                copy.wait_recv()

    def depart(copies):
        for _, inside, copy in copies:

            @pl.when(inside)
            def _():
                copy.wait_send()

    def pack(turn, edge):
        for half in range(2):
            first = edge[64 * half : 64 * half + 32]
            second = pltpu.roll(edge[64 * half + 32 : 64 * half + 64], 64, 1)
            rows_here = slice(32 * half, 32 * half + 32)
            pack_left[turn, rows_here, :] = jnp.where(lane, first, second)
            pack_right[turn, rows_here, :] = jnp.where(lane, second, first)

    def along_rows(which, value):
        high, low = split(value)
        both = dot(row_mats[which], high)
        return both[0:128] + both[128:256] + dot(row_mats[which, 0:128, :], low)

    def along_cols(which, blocks, first, second):
        height = blocks[first].shape[0]
        low_lanes = lane_tall if height == 128 else lane_deep
        nothing = jnp.zeros((height, 128), jnp.float32)
        pairs = []
        for b in (first, second):
            mixed = jnp.where(low_lanes, blocks.get(b + 1, nothing), blocks.get(b - 1, nothing))
            pairs.append(jnp.concatenate([blocks[b], mixed], axis=1))
        high, low = split(jnp.concatenate(pairs, axis=0))
        both = dot(high, col_mats[which])
        flat = both[:, 0:128] + both[:, 128:256] + dot(low, col_mats[which, :, 0:128])
        return flat[0:height], flat[height : 2 * height]

    def along_cols_edge(which, halo):
        high, low = split(halo)
        both = dot(high, col_mats[which, 128:256, :])
        return both[:, 0:128] + both[:, 128:256] + dot(low, col_mats[which, 128:256, 0:128])

    def along_rows_deep(which, value):
        return jnp.concatenate(
            [along_rows(which, value[0:256]), along_rows(which, value[128:384])], axis=0
        )

    def sides(turn):
        parts = []
        for group in range(4):
            from_left = left[turn, 32 * group : 32 * group + 32, :]
            from_right = right[turn, 32 * group : 32 * group + 32, :]
            parts.append(jnp.where(lane, from_right, from_left))
            parts.append(pltpu.roll(jnp.where(lane, from_left, from_right), 64, 1))
        return jnp.concatenate(parts, axis=0)

    def squares(difference):
        return jnp.sum(difference * difference, axis=0, keepdims=True)

    def norm_row(d):
        return pltpu.make_async_remote_copy(
            src_ref=partial,
            dst_ref=gather_rows.at[row],
            send_sem=norm_send.at[0],
            recv_sem=norm_recv.at[0],
            device_id=(lax.rem(row + d, rows), col),
            device_id_type=MESH,
        )

    def norm_col(d):
        return pltpu.make_async_remote_copy(
            src_ref=middle,
            dst_ref=gather_cols.at[col],
            send_sem=norm_send.at[1],
            recv_sem=norm_recv.at[1],
            device_id=(row, lax.rem(col + d, cols)),
            device_id_type=MESH,
        )

    def wait_all(buffer, count, semaphore):
        whole = buffer.at[pl.ds(0, count)]
        pltpu.make_async_copy(whole, whole, semaphore).wait()

    def start_norm_row(d, carry):
        norm_row(d).start()
        return carry

    def served(r, c):
        out = jnp.bool_(False)
        for e in early:
            out = out | ((r == e[0]) & (c == e[1]))
        return out

    def start_norm_col(d, carry):
        @pl.when(jnp.logical_not(served(row, lax.rem(col + d, cols))))
        def _():
            norm_col(d).start()

        return carry

    def direct(k):
        return pltpu.make_async_remote_copy(
            src_ref=partial,
            dst_ref=gather_all.at[row * cols + col],
            send_sem=norm_send.at[2 + k],
            recv_sem=norm_recv.at[2],
            device_id=early[k],
            device_id_type=MESH,
        )

    am_early = served(row, col)
    one_less = jnp.bool_(False)
    for e in early:
        one_less = one_less | ((row == e[0]) & (col != e[1]))

    def tell(level):
        for k, steps in enumerate(((1, 0), (0, 1))):
            if 1 << level < (rows, cols)[k] - 1:
                for sign in (-1, 1):
                    inside, device = near(tuple(sign * (1 << level) * s for s in steps))

                    @pl.when(inside)
                    def _():
                        pl.semaphore_signal(
                            known.at[level, k], inc=1, device_id=device, device_id_type=MESH
                        )

    def hear(level):
        for k, steps in enumerate(((1, 0), (0, 1))):
            if 1 << level < (rows, cols)[k] - 1:
                told = jnp.int32(0)
                for sign in (-1, 1):
                    inside, _ = near(tuple(sign * (1 << level) * s for s in steps))
                    told = told + inside.astype(jnp.int32)
                pl.semaphore_wait(known.at[level, k], told)

    load_start.wait()
    pack(0, jnp.where(lane_tall, field[0, 64:192, 0:128], field[0, 64:192, 384:512]))
    pl.semaphore_wait(barrier, expected)
    start(side_copies(0))
    start(row_copies(0, (0, 1, 2, 3)))
    tell(0)

    @pl.when(row == 0)
    def _():
        for k in (0, 2):
            field[k, 0:64, :] = jnp.zeros((64, 512), jnp.float32)
        ratio[0:128, :] = jnp.zeros((128, 512), jnp.float32)
        for buffer in (left, right):
            buffer[:, 0:32, :] = jnp.zeros((2, 32, 128), jnp.float32)
        for buffer in (deep_left, deep_right):
            buffer[0:128, :] = jnp.zeros((128, 128), jnp.float32)

    @pl.when(row == rows - 1)
    def _():
        for k in (0, 2):
            field[k, 192:256, :] = jnp.zeros((64, 512), jnp.float32)
        ratio[256:384, :] = jnp.zeros((128, 512), jnp.float32)
        for buffer in (left, right):
            buffer[:, 96:128, :] = jnp.zeros((2, 32, 128), jnp.float32)
        for buffer in (deep_left, deep_right):
            buffer[256:384, :] = jnp.zeros((128, 128), jnp.float32)

    @pl.when(col == 0)
    def _():
        left[...] = jnp.zeros((2, 128, 128), jnp.float32)
        deep_left[...] = jnp.zeros((384, 128), jnp.float32)

    @pl.when(col == cols - 1)
    def _():
        right[...] = jnp.zeros((2, 128, 128), jnp.float32)
        deep_right[...] = jnp.zeros((384, 128), jnp.float32)

    load_rows.wait()
    load_cols.wait()
    taps[...] = jnp.zeros((8, 256), jnp.float32)
    taps[0:1, 0:127] = taps_rows[...] / jnp.sum(taps_rows[...])
    taps[1:2, 0:127] = taps_cols[...] / jnp.sum(taps_cols[...])
    row_taps, col_taps = taps[0:1, :], taps[1:2, :]
    by_rows = (circulant(row_taps, 1, 128), circulant(row_taps, -127, 256)[:, :128].T)
    along = circulant(col_taps, -63, 256)
    by_cols = (along[:128].T, along[:, :128])
    for which in range(2):
        high, low = split(by_rows[which])
        row_mats[which, 0:128, :] = high
        row_mats[which, 128:256, :] = low
        high, low = split(by_cols[which])
        col_mats[which, :, 0:128] = high
        col_mats[which, :, 128:256] = low
    load_seen.wait()

    def at(b):
        return slice(128 * b, 128 * b + 128)

    def pair(value):
        return value[:, 0:128], value[:, 128:256]

    def outer_blocks(value):
        return jnp.concatenate([value[:, 0:128], value[:, 384:512]], axis=1)

    rounds = max(doublings(rows), doublings(cols))

    def spread(level):
        if level < rounds:
            hear(level)
            tell(level + 1)

    spread(0)

    blocks, outs = {}, {}
    arrive(row_copies(0, (1, 2)))
    blocks[1], blocks[2] = pair(along_rows(0, field[0, :, 128:384]))
    arrive(row_copies(0, (0, 3)))
    blocks[0], blocks[3] = pair(along_rows(0, outer_blocks(field[0])))
    outs[1], outs[2] = along_cols(0, blocks, 1, 2)
    for b in (1, 2):
        ratio[128:256, at(b)] = seen[:, at(b)] / outs[b]
    start(deep_row_copies((1, 2)))
    outs[0], outs[3] = along_cols(0, blocks, 0, 3)
    seen_edge = jnp.where(lane_tall, seen[:, at(0)], seen[:, at(3)])
    edge = jnp.where(lane_tall, outs[0], outs[3])
    for b in (0, 3):
        ratio[128:256, at(b)] = seen[:, at(b)] / outs[b]
    inner_sum = squares(seen[:, at(1)] - outs[1]) + squares(seen[:, at(2)] - outs[2])
    inner_sum = inner_sum + squares(
        jnp.where(lane_tall, seen[:, at(3)] - outs[3], seen[:, at(0)] - outs[0])
    )
    spread(1)
    arrive(side_copies(0))
    halo = sides(0)
    beside[...] = halo
    edge = edge + along_cols_edge(0, along_rows(0, halo))
    outer = seen_edge / edge
    ratio[128:256, at(0)] = jnp.where(lane_tall, outer, ratio[128:256, at(0)])
    ratio[128:256, at(3)] = jnp.where(lane_tall, ratio[128:256, at(3)], outer)
    start(deep_side_copies())
    start(deep_row_copies((0, 3)))
    first_norm = inner_sum + squares(seen_edge - edge)
    first_norm = first_norm + pltpu.roll(first_norm, 64, 1)
    spread(2)
    spread(3)

    blocks, outs = {}, {}
    arrive(deep_row_copies((1, 2)))
    blocks[1], blocks[2] = pair(along_rows_deep(1, ratio[:, 128:384]))
    arrive(deep_row_copies((0, 3)))
    blocks[0], blocks[3] = pair(along_rows_deep(1, outer_blocks(ratio)))
    outs[1], outs[2] = along_cols(1, blocks, 1, 2)
    for b in (1, 2):
        field[1, :, at(b)] = field[0, :, at(b)] * outs[b]
    outs[0], outs[3] = along_cols(1, blocks, 0, 3)
    again = {}
    again[1], again[2] = pair(along_rows(0, field[1, :, 128:384]))
    for level in range(4, rounds):
        spread(level)
    arrive(deep_side_copies())
    blocks[-1], blocks[4] = pair(
        along_rows_deep(1, jnp.concatenate([deep_left[...], deep_right[...]], axis=1))
    )
    edge = along_cols_edge(1, jnp.where(lane_deep, blocks[4], blocks[-1]))
    outs[-1], outs[4] = along_cols(1, blocks, -1, 4)
    field[1, :, at(0)] = field[0, :, at(0)] * jnp.where(lane_deep, outs[0] + edge, outs[0])
    field[1, :, at(3)] = field[0, :, at(3)] * jnp.where(lane_deep, outs[3], outs[3] + edge)
    halo = beside[...] * jnp.where(lane_deep, outs[4], outs[-1])

    again[0], again[3] = pair(along_rows(0, outer_blocks(field[1])))
    again[-1] = again[4] = along_rows(0, halo)
    outs = {}
    outs[0], outs[3] = along_cols(0, again, 0, 3)
    outs[1], outs[2] = along_cols(0, again, 1, 2)
    last_norm = sum(squares(seen[:, at(b)] - outs[b]) for b in range(4))
    last_norm = last_norm + pltpu.roll(last_norm, 64, 1)
    partial[...] = jnp.where(lane[0:1], first_norm, last_norm)
    gather_rows[row] = partial[...]
    for k, here in enumerate(is_early):

        @pl.when(here)
        def _():
            gather_all[row * cols + col] = partial[...]

        @pl.when(jnp.logical_not(here))
        def _():
            direct(k).start()

    lax.fori_loop(1, rows, start_norm_row, 0)
    for b in range(4):
        field[2, 64:192, at(b)] = seen[:, at(b)] / outs[b]
    pack(1, jnp.where(lane_tall, field[2, 64:192, at(0)], field[2, 64:192, at(3)]))
    start(side_copies(1))
    start(row_copies(1, (0, 1, 2, 3)))

    wait_all(gather_rows, rows - 1, norm_recv.at[0])
    total = gather_rows[0]
    for r in range(1, rows):
        total = total + gather_rows[r]
    middle[...] = total
    gather_cols[col] = total
    lax.fori_loop(1, cols, start_norm_col, 0)

    blocks, outs = {}, {}
    arrive(row_copies(1, (0, 1, 2, 3)))
    blocks[1], blocks[2] = pair(along_rows(1, field[2, :, 128:384]))
    blocks[0], blocks[3] = pair(along_rows(1, outer_blocks(field[2])))
    outs[1], outs[2] = along_cols(1, blocks, 1, 2)
    arrive(side_copies(1))
    blocks[-1] = blocks[4] = along_rows(1, sides(1))
    outs[0], outs[3] = along_cols(1, blocks, 0, 3)
    for b in range(4):
        result[:, at(b)] = field[1, 64:192, at(b)] * outs[b]

    store = pltpu.make_async_copy(result, out_ref, local.at[4])
    store.start()
    for turn in range(2):
        depart(side_copies(turn))
        depart(row_copies(turn, (0, 1, 2, 3)))
    depart(deep_side_copies())
    depart(deep_row_copies((0, 1, 2, 3)))
    wait_all(gather_rows, rows - 1, norm_send.at[0])
    place = lax.broadcasted_iota(jnp.int32, (1, 2), 1)

    def put_norms(total):
        first = jnp.sum(jnp.where(lane[0:1], total, 0.0), axis=1, keepdims=True)
        last = jnp.sum(jnp.where(lane[0:1], 0.0, total), axis=1, keepdims=True)
        norms_ref[...] = jnp.where(place == 0, first, last)

    @pl.when(am_early)
    def _():
        wait_all(gather_all, rows * cols - 1, norm_recv.at[2])
        total = None
        for c in range(cols):
            part = gather_all[c]
            for r in range(1, rows):
                part = part + gather_all[r * cols + c]
            total = part if total is None else total + part
        put_norms(total)

    @pl.when(jnp.logical_not(am_early))
    def _():
        wait_all(gather_cols, cols - 1, norm_recv.at[1])
        total = gather_cols[0]
        for c in range(1, cols):
            total = total + gather_cols[c]
        put_norms(total)

    @pl.when(one_less)
    def _():
        wait_all(gather_cols, cols - 2, norm_send.at[1])

    @pl.when(jnp.logical_not(one_less))
    def _():
        wait_all(gather_cols, cols - 1, norm_send.at[1])

    for k, here in enumerate(is_early):

        @pl.when(jnp.logical_not(here))
        def _():
            direct(k).wait_send()

    store.wait()


def finish(estimate, norms, out, out_norms, done):
    copies = (
        pltpu.make_async_copy(estimate, out, done.at[0]),
        pltpu.make_async_copy(norms, out_norms, done.at[1]),
    )
    for copy in copies:
        copy.start()
    for copy in copies:
        copy.wait()


def body(rows, cols, observed, start, psf_rows, psf_cols):
    f32, bf16 = jnp.float32, jnp.bfloat16
    estimate, norms = pl.pallas_call(
        functools.partial(kernel, rows, cols),
        out_shape=(
            jax.ShapeDtypeStruct((128, 512), f32),
            jax.ShapeDtypeStruct((1, 2), f32),
        ),
        in_specs=[
            pl.BlockSpec(memory_space=pltpu.HBM),
            pl.BlockSpec(memory_space=pltpu.HBM),
            pl.BlockSpec(memory_space=pltpu.HBM),
            pl.BlockSpec(memory_space=pltpu.HBM),
        ],
        out_specs=(
            pl.BlockSpec(memory_space=pl.ANY),
            pl.BlockSpec(memory_space=pltpu.VMEM),
        ),
        scratch_shapes=[
            pltpu.VMEM((3, 256, 512), f32),
            pltpu.VMEM((2, 128, 128), f32),
            pltpu.VMEM((2, 128, 128), f32),
            pltpu.VMEM((2, 64, 128), f32),
            pltpu.VMEM((2, 64, 128), f32),
            pltpu.VMEM((256, 128), f32),
            pltpu.VMEM((384, 512), f32),
            pltpu.VMEM((384, 128), f32),
            pltpu.VMEM((384, 128), f32),
            pltpu.VMEM((128, 512), f32),
            pltpu.VMEM((128, 512), f32),
            pltpu.VMEM((1, 127), f32),
            pltpu.VMEM((1, 127), f32),
            pltpu.VMEM((8, 256), f32),
            pltpu.VMEM((2, 256, 256), bf16),
            pltpu.VMEM((2, 256, 256), bf16),
            pltpu.VMEM((1, 128), f32),
            pltpu.VMEM((rows, 1, 128), f32),
            pltpu.VMEM((1, 128), f32),
            pltpu.VMEM((cols, 1, 128), f32),
            pltpu.VMEM((rows * cols, 1, 128), f32),
            pltpu.SemaphoreType.DMA((3, 6)),
            pltpu.SemaphoreType.DMA((3, 6)),
            pltpu.SemaphoreType.DMA((3, 2, 4)),
            pltpu.SemaphoreType.DMA((3, 2, 4)),
            pltpu.SemaphoreType.DMA((5,)),
            pltpu.SemaphoreType.DMA((2 + len(EARLY),)),
            pltpu.SemaphoreType.DMA((3,)),
            pltpu.SemaphoreType.REGULAR((max(doublings(rows), doublings(cols)), 2)),
        ],
        compiler_params=pltpu.CompilerParams(
            collective_id=0, has_side_effects=True, vmem_limit_bytes=54850 * 1024
        ),
        name="deconvolve",
    )(observed[0], start[0], psf_rows.reshape(1, 127), psf_cols.reshape(1, 127))
    estimate, norms = pl.pallas_call(
        finish,
        out_shape=(jax.ShapeDtypeStruct((128, 512), f32), jax.ShapeDtypeStruct((1, 2), f32)),
        in_specs=[pl.BlockSpec(memory_space=pl.ANY)] * 2,
        out_specs=[pl.BlockSpec(memory_space=pl.ANY)] * 2,
        scratch_shapes=[
            pltpu.SemaphoreType.DMA((2,)),
        ],
        compiler_params=pltpu.CompilerParams(vmem_limit_bytes=54850 * 1024),
        name="finish",
    )(estimate, norms)
    return estimate[None], norms.reshape(2)


def solution(mesh):
    in_specs = (P(None, "row", "col"), P(None, "row", "col"), P(), P())
    out_specs = (P(None, "row", "col"), P())
    step = functools.partial(body, mesh.shape["row"], mesh.shape["col"])
    return jax.shard_map(step, mesh=mesh, in_specs=in_specs, out_specs=out_specs, check_vma=False)
```

```python
import functools

import jax
import jax.numpy as jnp
from jax import lax
from jax.experimental import pallas as pl
from jax.experimental.pallas import tpu as pltpu
from jax.sharding import PartitionSpec as P

MESH = pl.DeviceIdType.MESH
EARLY = ((1, 0), (2, 0), (16, 0), (0, 1))
SIDES = ((-1, -1), (-1, 1), (1, -1), (1, 1), (0, -1), (0, 1))
ENDS = ((-1, 0), (1, 0))


def split(value):
    high = value.astype(jnp.bfloat16)
    low = (value - high.astype(jnp.float32)).astype(jnp.bfloat16)
    return high, low


def dot(left, right):
    return jnp.dot(left, right, preferred_element_type=jnp.float32)


def circulant(taps, shift, rows):
    wide = jnp.broadcast_to(taps, (rows, 256))
    return pltpu.roll(wide, shift % 256, 1, stride=1, stride_axis=0)


def doublings(count):
    return max(count - 2, 0).bit_length()


def kernel(
    rows, cols, obs_hbm, start_hbm, rows_hbm, cols_hbm, out_ref, norms_ref,
    field, left, right, pack_left, pack_right, beside, ratio, deep_left, deep_right,
    seen, result, taps_rows, taps_cols, taps,
    row_mats, col_mats, partial, gather_rows, middle, gather_cols, gather_all,
    send_sides, recv_sides, send_rows, recv_rows, local, norm_send, norm_recv, known,
):
    row, col = lax.axis_index("row"), lax.axis_index("col")

    load_start = pltpu.make_async_copy(start_hbm, field.at[0, pl.ds(64, 128)], local.at[0])
    load_seen = pltpu.make_async_copy(obs_hbm, seen, local.at[1])
    load_rows = pltpu.make_async_copy(rows_hbm, taps_rows, local.at[2])
    load_cols = pltpu.make_async_copy(cols_hbm, taps_cols, local.at[3])
    load_start.start()

    def near(step):
        r, c = row + step[0], col + step[1]
        inside = (r >= 0) & (r < rows) & (c >= 0) & (c < cols)
        return inside, (r, c)

    barrier = pltpu.get_barrier_semaphore()
    expected = jnp.int32(0)
    for step in SIDES + ENDS:
        inside, device = near(step)

        @pl.when(inside)
        def _():
            pl.semaphore_signal(barrier, inc=1, device_id=device, device_id_type=MESH)

        expected = expected + inside.astype(jnp.int32)

    early = [(r, c) for r, c in EARLY if r < rows and c < cols]
    is_early = [(row == r) & (col == c) for r, c in early]
    for here in is_early:
        @pl.when(here)
        def _():
            def greet(k, carry):
                r, c = lax.rem(k, rows), cols - 1 - lax.div(k, rows)

                @pl.when((r != row) | (c != col))
                def _():
                    pl.semaphore_signal(
                        barrier, inc=1, device_id=(r, c), device_id_type=MESH
                    )

                return carry

            lax.fori_loop(0, rows * cols, greet, 0)

        expected = expected + (1 - here.astype(jnp.int32))

    load_seen.start()
    load_rows.start()
    load_cols.start()

    lane = lax.broadcasted_iota(jnp.int32, (32, 128), 1) < 64
    lane_tall = lax.broadcasted_iota(jnp.int32, (128, 128), 1) < 64
    lane_deep = lax.broadcasted_iota(jnp.int32, (256, 128), 1) < 64

    def remote(step, source, target, sent, received):
        inside, device = near(step)
        copy = pltpu.make_async_remote_copy(
            src_ref=source,
            dst_ref=target,
            send_sem=sent,
            recv_sem=received,
            device_id=device,
            device_id_type=MESH,
        )
        return step, inside, copy

    def side_copies(turn):
        ends = {
            (0, -1): (pack_left.at[turn], right.at[turn, pl.ds(32, 64)]),
            (0, 1): (pack_right.at[turn], left.at[turn, pl.ds(32, 64)]),
            (-1, -1): (pack_left.at[turn, pl.ds(0, 32)], right.at[turn, pl.ds(96, 32)]),
            (-1, 1): (pack_right.at[turn, pl.ds(0, 32)], left.at[turn, pl.ds(96, 32)]),
            (1, -1): (pack_left.at[turn, pl.ds(32, 32)], right.at[turn, pl.ds(0, 32)]),
            (1, 1): (pack_right.at[turn, pl.ds(32, 32)], left.at[turn, pl.ds(0, 32)]),
        }
        return [
            remote(step, *ends[step], send_sides.at[turn, k], recv_sides.at[turn, k])
            for k, step in enumerate(SIDES)
        ]

    def row_copies(turn):
        return [
            remote(
                step,
                field.at[2 * turn, pl.ds(source, 64)],
                field.at[2 * turn, pl.ds(target, 64)],
                send_rows.at[turn, k, 0],
                recv_rows.at[turn, k, 0],
            )
            for k, (step, source, target) in enumerate(((ENDS[0], 64, 192), (ENDS[1], 128, 0)))
        ]

    def deep_side_copies():
        made = []
        for k, (down, across) in enumerate(SIDES):
            block, target = (0, deep_right) if across < 0 else (3, deep_left)
            made.append(
                remote(
                    (down, across),
                    ratio.at[pl.ds(128, 128), pl.ds(128 * block, 128)],
                    target.at[pl.ds(128 - 128 * down, 128)],
                    send_sides.at[2, k],
                    recv_sides.at[2, k],
                )
            )
        return made

    def deep_row_copies(blocks):
        made = []
        for k, step in enumerate(ENDS):
            for b in blocks:
                lanes = pl.ds(128 * b, 128)
                made.append(
                    remote(
                        step,
                        ratio.at[pl.ds(128, 128), lanes],
                        ratio.at[pl.ds(128 - 128 * step[0], 128), lanes],
                        send_rows.at[2, k, b],
                        recv_rows.at[2, k, b],
                    )
                )
        return made

    def by_step(copies):
        groups = {}
        for step, inside, copy in copies:
            groups.setdefault(step, (inside, []))[1].append(copy)
        return groups.items()

    def start(copies):
        for _, (inside, group) in by_step(copies):

            @pl.when(inside)
            def _():
                for copy in group:
                    copy.start()

    def arrive(copies):
        for step, (_, group) in by_step(copies):
            inside, _ = near((-step[0], -step[1]))

            @pl.when(inside)
            def _():
                for copy in group:
                    copy.wait_recv()

    def depart(copies):
        for _, (inside, group) in by_step(copies):

            @pl.when(inside)
            def _():
                for copy in group:
                    copy.wait_send()

    def pack(turn, edge):
        for half in range(2):
            first = edge[64 * half : 64 * half + 32]
            second = pltpu.roll(edge[64 * half + 32 : 64 * half + 64], 64, 1)
            rows_here = slice(32 * half, 32 * half + 32)
            pack_left[turn, rows_here, :] = jnp.where(lane, first, second)
            pack_right[turn, rows_here, :] = jnp.where(lane, second, first)

    def along_rows(which, value):
        high, low = split(value)
        both = dot(row_mats[which], high)
        return both[0:128] + both[128:256] + dot(row_mats[which, 0:128, :], low)

    def along_cols(which, blocks, *wanted):
        height = blocks[wanted[0]].shape[0]
        low_lanes = lane_tall if height == 128 else lane_deep
        nothing = jnp.zeros((height, 128), jnp.float32)
        pairs = []
        for b in wanted:
            mixed = jnp.where(low_lanes, blocks.get(b + 1, nothing), blocks.get(b - 1, nothing))
            pairs.append(jnp.concatenate([blocks[b], mixed], axis=1))
        high, low = split(jnp.concatenate(pairs, axis=0))
        both = dot(high, col_mats[which])
        flat = both[:, 0:128] + both[:, 128:256] + dot(low, col_mats[which, :, 0:128])
        return [flat[height * k : height * (k + 1)] for k in range(len(wanted))]

    def along_cols_edge(which, halo):
        high, low = split(halo)
        both = dot(high, col_mats[which, 128:256, :])
        return both[:, 0:128] + both[:, 128:256] + dot(low, col_mats[which, 128:256, 0:128])

    def along_rows_deep(which, value):
        return jnp.concatenate(
            [along_rows(which, value[0:256]), along_rows(which, value[128:384])], axis=0
        )

    def sides(turn):
        parts = []
        for group in range(4):
            from_left = left[turn, 32 * group : 32 * group + 32, :]
            from_right = right[turn, 32 * group : 32 * group + 32, :]
            parts.append(jnp.where(lane, from_right, from_left))
            parts.append(pltpu.roll(jnp.where(lane, from_left, from_right), 64, 1))
        return jnp.concatenate(parts, axis=0)

    def squares(difference):
        return jnp.sum(difference * difference, axis=0, keepdims=True)

    def norm_row(d):
        return pltpu.make_async_remote_copy(
            src_ref=partial,
            dst_ref=gather_rows.at[row],
            send_sem=norm_send.at[0],
            recv_sem=norm_recv.at[0],
            device_id=(lax.rem(row + d, rows), col),
            device_id_type=MESH,
        )

    def norm_col(d):
        return pltpu.make_async_remote_copy(
            src_ref=middle,
            dst_ref=gather_cols.at[col],
            send_sem=norm_send.at[1],
            recv_sem=norm_recv.at[1],
            device_id=(row, lax.rem(col + d, cols)),
            device_id_type=MESH,
        )

    def wait_all(buffer, count, semaphore):
        whole = buffer.at[pl.ds(0, count)]
        pltpu.make_async_copy(whole, whole, semaphore).wait()

    def start_norm_row(d, carry):
        norm_row(d).start()
        return carry

    def served(r, c):
        out = jnp.bool_(False)
        for e in early:
            out = out | ((r == e[0]) & (c == e[1]))
        return out

    def start_norm_col(d, carry):
        @pl.when(jnp.logical_not(served(row, lax.rem(col + d, cols))))
        def _():
            norm_col(d).start()

        return carry

    def direct(k):
        return pltpu.make_async_remote_copy(
            src_ref=partial,
            dst_ref=gather_all.at[row * cols + col],
            send_sem=norm_send.at[2 + k],
            recv_sem=norm_recv.at[2],
            device_id=early[k],
            device_id_type=MESH,
        )

    am_early = served(row, col)
    one_less = jnp.bool_(False)
    for e in early:
        one_less = one_less | ((row == e[0]) & (col != e[1]))

    def tell(level):
        for k, steps in enumerate(((1, 0), (0, 1))):
            if 1 << level < (rows, cols)[k] - 1:
                for sign in (-1, 1):
                    inside, device = near(tuple(sign * (1 << level) * s for s in steps))

                    @pl.when(inside)
                    def _():
                        pl.semaphore_signal(
                            known.at[level, k], inc=1, device_id=device, device_id_type=MESH
                        )

    def hear(level):
        for k, steps in enumerate(((1, 0), (0, 1))):
            if 1 << level < (rows, cols)[k] - 1:
                told = jnp.int32(0)
                for sign in (-1, 1):
                    inside, _ = near(tuple(sign * (1 << level) * s for s in steps))
                    told = told + inside.astype(jnp.int32)
                pl.semaphore_wait(known.at[level, k], told)

    load_start.wait()
    pack(0, jnp.where(lane_tall, field[0, 64:192, 0:128], field[0, 64:192, 384:512]))
    pl.semaphore_wait(barrier, expected)
    start(side_copies(0))
    start(row_copies(0))
    tell(0)

    @pl.when(row == 0)
    def _():
        for k in (0, 2):
            field[k, 0:64, :] = jnp.zeros((64, 512), jnp.float32)
        ratio[0:128, :] = jnp.zeros((128, 512), jnp.float32)
        for buffer in (left, right):
            buffer[:, 0:32, :] = jnp.zeros((2, 32, 128), jnp.float32)
        for buffer in (deep_left, deep_right):
            buffer[0:128, :] = jnp.zeros((128, 128), jnp.float32)

    @pl.when(row == rows - 1)
    def _():
        for k in (0, 2):
            field[k, 192:256, :] = jnp.zeros((64, 512), jnp.float32)
        ratio[256:384, :] = jnp.zeros((128, 512), jnp.float32)
        for buffer in (left, right):
            buffer[:, 96:128, :] = jnp.zeros((2, 32, 128), jnp.float32)
        for buffer in (deep_left, deep_right):
            buffer[256:384, :] = jnp.zeros((128, 128), jnp.float32)

    @pl.when(col == 0)
    def _():
        left[...] = jnp.zeros((2, 128, 128), jnp.float32)
        deep_left[...] = jnp.zeros((384, 128), jnp.float32)

    @pl.when(col == cols - 1)
    def _():
        right[...] = jnp.zeros((2, 128, 128), jnp.float32)
        deep_right[...] = jnp.zeros((384, 128), jnp.float32)

    load_rows.wait()
    load_cols.wait()
    taps[...] = jnp.zeros((8, 256), jnp.float32)
    taps[0:1, 0:127] = taps_rows[...] / jnp.sum(taps_rows[...])
    taps[1:2, 0:127] = taps_cols[...] / jnp.sum(taps_cols[...])
    row_taps, col_taps = taps[0:1, :], taps[1:2, :]
    by_rows = (circulant(row_taps, 1, 128), circulant(row_taps, -127, 256)[:, :128].T)
    along = circulant(col_taps, -63, 256)
    by_cols = (along[:128].T, along[:, :128])
    for which in range(2):
        high, low = split(by_rows[which])
        row_mats[which, 0:128, :] = high
        row_mats[which, 128:256, :] = low
        high, low = split(by_cols[which])
        col_mats[which, :, 0:128] = high
        col_mats[which, :, 128:256] = low
    load_seen.wait()

    def at(b):
        return slice(128 * b, 128 * b + 128)

    def pair(value):
        return value[:, 0:128], value[:, 128:256]

    def outer_blocks(value):
        return jnp.concatenate([value[:, 0:128], value[:, 384:512]], axis=1)

    rounds = max(doublings(rows), doublings(cols))

    def spread(level):
        if level < rounds:
            hear(level)
            tell(level + 1)

    spread(0)

    blocks, outs = {}, {}
    arrive(row_copies(0))
    blocks[1], blocks[2] = pair(along_rows(0, field[0, :, 128:384]))
    blocks[0], blocks[3] = pair(along_rows(0, outer_blocks(field[0])))
    outs[1], outs[2] = along_cols(0, blocks, 1, 2)
    for b in (1, 2):
        ratio[128:256, at(b)] = seen[:, at(b)] / outs[b]
    start(deep_row_copies((1, 2)))
    outs[0], outs[3] = along_cols(0, blocks, 0, 3)
    seen_edge = jnp.where(lane_tall, seen[:, at(0)], seen[:, at(3)])
    edge = jnp.where(lane_tall, outs[0], outs[3])
    for b in (0, 3):
        ratio[128:256, at(b)] = seen[:, at(b)] / outs[b]
    inner_sum = squares(seen[:, at(1)] - outs[1]) + squares(seen[:, at(2)] - outs[2])
    inner_sum = inner_sum + squares(
        jnp.where(lane_tall, seen[:, at(3)] - outs[3], seen[:, at(0)] - outs[0])
    )
    spread(1)
    arrive(side_copies(0))
    halo = sides(0)
    beside[...] = halo
    edge = edge + along_cols_edge(0, along_rows(0, halo))
    outer = seen_edge / edge
    ratio[128:256, at(0)] = jnp.where(lane_tall, outer, ratio[128:256, at(0)])
    ratio[128:256, at(3)] = jnp.where(lane_tall, ratio[128:256, at(3)], outer)
    start(deep_side_copies())
    start(deep_row_copies((0, 3)))
    first_norm = inner_sum + squares(seen_edge - edge)
    first_norm = first_norm + pltpu.roll(first_norm, 64, 1)
    spread(2)
    spread(3)

    blocks, outs = {}, {}
    arrive(deep_row_copies((1, 2)))
    blocks[1], blocks[2] = pair(along_rows_deep(1, ratio[:, 128:384]))
    arrive(deep_row_copies((0, 3)))
    blocks[0], blocks[3] = pair(along_rows_deep(1, outer_blocks(ratio)))
    outs[1], outs[2] = along_cols(1, blocks, 1, 2)
    for b in (1, 2):
        field[1, :, at(b)] = field[0, :, at(b)] * outs[b]
    outs[0], outs[3] = along_cols(1, blocks, 0, 3)
    again = {}
    again[1], again[2] = pair(along_rows(0, field[1, :, 128:384]))
    for level in range(4, rounds):
        spread(level)
    arrive(deep_side_copies())
    blocks[-1], blocks[4] = pair(
        along_rows_deep(1, jnp.concatenate([deep_left[...], deep_right[...]], axis=1))
    )
    edge = along_cols_edge(1, jnp.where(lane_deep, blocks[4], blocks[-1]))
    outs[-1], outs[4] = along_cols(1, blocks, -1, 4)
    first = field[0, :, at(0)] * jnp.where(lane_deep, outs[0] + edge, outs[0])
    fourth = field[0, :, at(3)] * jnp.where(lane_deep, outs[3], outs[3] + edge)
    field[1, :, at(0)] = first
    field[1, :, at(3)] = fourth
    halo = beside[...] * jnp.where(lane_deep, outs[4], outs[-1])

    both = along_rows(0, jnp.concatenate([first, fourth, halo], axis=1))
    again[0], again[3] = pair(both)
    again[-1] = again[4] = both[:, 256:384]
    outs = along_cols(0, again, 0, 1, 2, 3)
    last_norm = sum(squares(seen[:, at(b)] - outs[b]) for b in range(4))
    last_norm = last_norm + pltpu.roll(last_norm, 64, 1)
    partial[...] = jnp.where(lane[0:1], first_norm, last_norm)
    gather_rows[row] = partial[...]
    for k, here in enumerate(is_early):

        @pl.when(here)
        def _():
            gather_all[row * cols + col] = partial[...]

        @pl.when(jnp.logical_not(here))
        def _():
            direct(k).start()

    lax.fori_loop(1, rows, start_norm_row, 0)
    for b in range(4):
        field[2, 64:192, at(b)] = seen[:, at(b)] / outs[b]
    pack(1, jnp.where(lane_tall, field[2, 64:192, at(0)], field[2, 64:192, at(3)]))
    start(side_copies(1))
    start(row_copies(1))

    wait_all(gather_rows, rows - 1, norm_recv.at[0])
    total = gather_rows[0]
    for r in range(1, rows):
        total = total + gather_rows[r]
    middle[...] = total
    gather_cols[col] = total
    lax.fori_loop(1, cols, start_norm_col, 0)

    blocks, outs = {}, {}
    arrive(row_copies(1))
    blocks[1], blocks[2] = pair(along_rows(1, field[2, :, 128:384]))
    blocks[0], blocks[3] = pair(along_rows(1, outer_blocks(field[2])))
    outs[1], outs[2] = along_cols(1, blocks, 1, 2)
    arrive(side_copies(1))
    blocks[-1] = blocks[4] = along_rows(1, sides(1))
    outs[0], outs[3] = along_cols(1, blocks, 0, 3)
    for b in range(4):
        result[:, at(b)] = field[1, 64:192, at(b)] * outs[b]

    store = pltpu.make_async_copy(result, out_ref, local.at[4])
    store.start()
    for turn in range(2):
        depart(side_copies(turn))
        depart(row_copies(turn))
    depart(deep_side_copies())
    depart(deep_row_copies((0, 1, 2, 3)))
    wait_all(gather_rows, rows - 1, norm_send.at[0])
    place = lax.broadcasted_iota(jnp.int32, (1, 2), 1)

    def put_norms(total):
        first = jnp.sum(jnp.where(lane[0:1], total, 0.0), axis=1, keepdims=True)
        last = jnp.sum(jnp.where(lane[0:1], 0.0, total), axis=1, keepdims=True)
        norms_ref[...] = jnp.where(place == 0, first, last)

    @pl.when(am_early)
    def _():
        wait_all(gather_all, rows * cols - 1, norm_recv.at[2])
        total = None
        for c in range(cols):
            part = gather_all[c]
            for r in range(1, rows):
                part = part + gather_all[r * cols + c]
            total = part if total is None else total + part
        put_norms(total)

    @pl.when(jnp.logical_not(am_early))
    def _():
        wait_all(gather_cols, cols - 1, norm_recv.at[1])
        total = gather_cols[0]
        for c in range(1, cols):
            total = total + gather_cols[c]
        put_norms(total)

    @pl.when(one_less)
    def _():
        wait_all(gather_cols, cols - 2, norm_send.at[1])

    @pl.when(jnp.logical_not(one_less))
    def _():
        wait_all(gather_cols, cols - 1, norm_send.at[1])

    for k, here in enumerate(is_early):

        @pl.when(jnp.logical_not(here))
        def _():
            direct(k).wait_send()

    store.wait()


def finish(estimate, norms, out, out_norms, done):
    copies = (
        pltpu.make_async_copy(estimate, out, done.at[0]),
        pltpu.make_async_copy(norms, out_norms, done.at[1]),
    )
    for copy in copies:
        copy.start()
    for copy in copies:
        copy.wait()


def body(rows, cols, observed, start, psf_rows, psf_cols):
    f32, bf16 = jnp.float32, jnp.bfloat16
    estimate, norms = pl.pallas_call(
        functools.partial(kernel, rows, cols),
        out_shape=(
            jax.ShapeDtypeStruct((128, 512), f32),
            jax.ShapeDtypeStruct((1, 2), f32),
        ),
        in_specs=[
            pl.BlockSpec(memory_space=pltpu.HBM),
            pl.BlockSpec(memory_space=pltpu.HBM),
            pl.BlockSpec(memory_space=pltpu.HBM),
            pl.BlockSpec(memory_space=pltpu.HBM),
        ],
        out_specs=(
            pl.BlockSpec(memory_space=pl.ANY),
            pl.BlockSpec(memory_space=pltpu.VMEM),
        ),
        scratch_shapes=[
            pltpu.VMEM((3, 256, 512), f32),
            pltpu.VMEM((2, 128, 128), f32),
            pltpu.VMEM((2, 128, 128), f32),
            pltpu.VMEM((2, 64, 128), f32),
            pltpu.VMEM((2, 64, 128), f32),
            pltpu.VMEM((256, 128), f32),
            pltpu.VMEM((384, 512), f32),
            pltpu.VMEM((384, 128), f32),
            pltpu.VMEM((384, 128), f32),
            pltpu.VMEM((128, 512), f32),
            pltpu.VMEM((128, 512), f32),
            pltpu.VMEM((1, 127), f32),
            pltpu.VMEM((1, 127), f32),
            pltpu.VMEM((8, 256), f32),
            pltpu.VMEM((2, 256, 256), bf16),
            pltpu.VMEM((2, 256, 256), bf16),
            pltpu.VMEM((1, 128), f32),
            pltpu.VMEM((rows, 1, 128), f32),
            pltpu.VMEM((1, 128), f32),
            pltpu.VMEM((cols, 1, 128), f32),
            pltpu.VMEM((rows * cols, 1, 128), f32),
            pltpu.SemaphoreType.DMA((3, 6)),
            pltpu.SemaphoreType.DMA((3, 6)),
            pltpu.SemaphoreType.DMA((3, 2, 4)),
            pltpu.SemaphoreType.DMA((3, 2, 4)),
            pltpu.SemaphoreType.DMA((5,)),
            pltpu.SemaphoreType.DMA((2 + len(EARLY),)),
            pltpu.SemaphoreType.DMA((3,)),
            pltpu.SemaphoreType.REGULAR((max(doublings(rows), doublings(cols)), 2)),
        ],
        compiler_params=pltpu.CompilerParams(
            collective_id=0, has_side_effects=True, vmem_limit_bytes=54850 * 1024
        ),
        name="deconvolve",
    )(observed[0], start[0], psf_rows.reshape(1, 127), psf_cols.reshape(1, 127))
    estimate, norms = pl.pallas_call(
        finish,
        out_shape=(jax.ShapeDtypeStruct((128, 512), f32), jax.ShapeDtypeStruct((1, 2), f32)),
        in_specs=[pl.BlockSpec(memory_space=pl.ANY)] * 2,
        out_specs=[pl.BlockSpec(memory_space=pl.ANY)] * 2,
        scratch_shapes=[
            pltpu.SemaphoreType.DMA((2,)),
        ],
        compiler_params=pltpu.CompilerParams(vmem_limit_bytes=54850 * 1024),
        name="finish",
    )(estimate, norms)
    return estimate[None], norms.reshape(2)


def solution(mesh):
    in_specs = (P(None, "row", "col"), P(None, "row", "col"), P(), P())
    out_specs = (P(None, "row", "col"), P())
    step = functools.partial(body, mesh.shape["row"], mesh.shape["col"])
    return jax.shard_map(step, mesh=mesh, in_specs=in_specs, out_specs=out_specs, check_vma=False)
```

```python
import functools

import jax
import jax.numpy as jnp
from jax import lax
from jax.experimental import pallas as pl
from jax.experimental.pallas import tpu as pltpu
from jax.sharding import PartitionSpec as P

MESH = pl.DeviceIdType.MESH
EARLY = ((1, 0), (2, 0), (16, 0), (0, 1))
SIDES = ((-1, -1), (-1, 1), (1, -1), (1, 1), (0, -1), (0, 1))
ENDS = ((-1, 0), (1, 0))


def split(value):
    high = value.astype(jnp.bfloat16)
    low = (value - high.astype(jnp.float32)).astype(jnp.bfloat16)
    return high, low


def dot(left, right):
    return jnp.dot(left, right, preferred_element_type=jnp.float32)


def circulant(taps, shift, rows):
    wide = jnp.broadcast_to(taps, (rows, 256))
    return pltpu.roll(wide, shift % 256, 1, stride=1, stride_axis=0)


def doublings(count):
    return max(count - 2, 0).bit_length()


def kernel(
    rows, cols, obs_hbm, start_hbm, rows_hbm, cols_hbm, out_ref, norms_ref,
    field, left, right, pack_left, pack_right, beside, ratio, deep_left, deep_right,
    seen, result, taps_rows, taps_cols, taps,
    row_mats, col_mats, partial, gather_rows, middle, gather_cols, gather_all,
    send_sides, recv_sides, send_rows, recv_rows, local, norm_send, norm_recv, known,
):
    row, col = lax.axis_index("row"), lax.axis_index("col")

    load_start = pltpu.make_async_copy(start_hbm, field.at[0, pl.ds(64, 128)], local.at[0])
    load_seen = pltpu.make_async_copy(obs_hbm, seen, local.at[1])
    load_rows = pltpu.make_async_copy(rows_hbm, taps_rows, local.at[2])
    load_cols = pltpu.make_async_copy(cols_hbm, taps_cols, local.at[3])
    load_start.start()

    def near(step):
        r, c = row + step[0], col + step[1]
        inside = (r >= 0) & (r < rows) & (c >= 0) & (c < cols)
        return inside, (r, c)

    barrier = pltpu.get_barrier_semaphore()
    expected = jnp.int32(0)
    for step in SIDES + ENDS:
        inside, device = near(step)

        @pl.when(inside)
        def _():
            pl.semaphore_signal(barrier, inc=1, device_id=device, device_id_type=MESH)

        expected = expected + inside.astype(jnp.int32)

    early = [(r, c) for r, c in EARLY if r < rows and c < cols]
    is_early = [(row == r) & (col == c) for r, c in early]
    for here in is_early:
        @pl.when(here)
        def _():
            def greet(k, carry):
                r, c = lax.rem(k, rows), cols - 1 - lax.div(k, rows)

                @pl.when((r != row) | (c != col))
                def _():
                    pl.semaphore_signal(
                        barrier, inc=1, device_id=(r, c), device_id_type=MESH
                    )

                return carry

            lax.fori_loop(0, rows * cols, greet, 0)

        expected = expected + (1 - here.astype(jnp.int32))

    load_seen.start()
    load_rows.start()
    load_cols.start()

    lane = lax.broadcasted_iota(jnp.int32, (32, 128), 1) < 64
    lane_tall = lax.broadcasted_iota(jnp.int32, (128, 128), 1) < 64
    lane_deep = lax.broadcasted_iota(jnp.int32, (256, 128), 1) < 64

    def remote(step, source, target, sent, received):
        inside, device = near(step)
        copy = pltpu.make_async_remote_copy(
            src_ref=source,
            dst_ref=target,
            send_sem=sent,
            recv_sem=received,
            device_id=device,
            device_id_type=MESH,
        )
        return step, inside, copy

    def side_copies(turn):
        ends = {
            (0, -1): (pack_left.at[turn], right.at[turn, pl.ds(32, 64)]),
            (0, 1): (pack_right.at[turn], left.at[turn, pl.ds(32, 64)]),
            (-1, -1): (pack_left.at[turn, pl.ds(0, 32)], right.at[turn, pl.ds(96, 32)]),
            (-1, 1): (pack_right.at[turn, pl.ds(0, 32)], left.at[turn, pl.ds(96, 32)]),
            (1, -1): (pack_left.at[turn, pl.ds(32, 32)], right.at[turn, pl.ds(0, 32)]),
            (1, 1): (pack_right.at[turn, pl.ds(32, 32)], left.at[turn, pl.ds(0, 32)]),
        }
        return [
            remote(step, *ends[step], send_sides.at[turn, k], recv_sides.at[turn, k])
            for k, step in enumerate(SIDES)
        ]

    def row_copies(turn, blocks):
        made = []
        for k, step in enumerate(ENDS):
            source, target = ((64, 192), (128, 0))[k]
            for b in blocks:
                lanes = pl.ds(128 * b, 128)
                made.append(
                    remote(
                        step,
                        field.at[2 * turn, pl.ds(source, 64), lanes],
                        field.at[2 * turn, pl.ds(target, 64), lanes],
                        send_rows.at[turn, k, b],
                        recv_rows.at[turn, k, b],
                    )
                )
        return made

    def deep_side_copies():
        made = []
        for k, (down, across) in enumerate(SIDES):
            block, target = (0, deep_right) if across < 0 else (3, deep_left)
            made.append(
                remote(
                    (down, across),
                    ratio.at[pl.ds(128, 128), pl.ds(128 * block, 128)],
                    target.at[pl.ds(128 - 128 * down, 128)],
                    send_sides.at[2, k],
                    recv_sides.at[2, k],
                )
            )
        return made

    def deep_row_copies(blocks):
        made = []
        for k, step in enumerate(ENDS):
            for b in blocks:
                lanes = pl.ds(128 * b, 128)
                made.append(
                    remote(
                        step,
                        ratio.at[pl.ds(128, 128), lanes],
                        ratio.at[pl.ds(128 - 128 * step[0], 128), lanes],
                        send_rows.at[2, k, b],
                        recv_rows.at[2, k, b],
                    )
                )
        return made

    def start(copies):
        for _, inside, copy in copies:

            @pl.when(inside)
            def _():
                copy.start()

    def arrive(copies):
        for step, _, copy in copies:
            inside, _ = near((-step[0], -step[1]))

            @pl.when(inside)
            def _():
                copy.wait_recv()

    def depart(copies):
        for _, inside, copy in copies:

            @pl.when(inside)
            def _():
                copy.wait_send()

    def pack(turn, edge):
        for half in range(2):
            first = edge[64 * half : 64 * half + 32]
            second = pltpu.roll(edge[64 * half + 32 : 64 * half + 64], 64, 1)
            rows_here = slice(32 * half, 32 * half + 32)
            pack_left[turn, rows_here, :] = jnp.where(lane, first, second)
            pack_right[turn, rows_here, :] = jnp.where(lane, second, first)

    def along_rows(which, value):
        high, low = split(value)
        both = dot(row_mats[which], high)
        return both[0:128] + both[128:256] + dot(row_mats[which, 0:128, :], low)

    def along_cols(which, blocks, first, second):
        height = blocks[first].shape[0]
        low_lanes = lane_tall if height == 128 else lane_deep
        nothing = jnp.zeros((height, 128), jnp.float32)
        pairs = []
        for b in (first, second):
            mixed = jnp.where(low_lanes, blocks.get(b + 1, nothing), blocks.get(b - 1, nothing))
            pairs.append(jnp.concatenate([blocks[b], mixed], axis=1))
        high, low = split(jnp.concatenate(pairs, axis=0))
        both = dot(high, col_mats[which])
        flat = both[:, 0:128] + both[:, 128:256] + dot(low, col_mats[which, :, 0:128])
        return flat[0:height], flat[height : 2 * height]

    def along_cols_edge(which, halo):
        high, low = split(halo)
        both = dot(high, col_mats[which, 128:256, :])
        return both[:, 0:128] + both[:, 128:256] + dot(low, col_mats[which, 128:256, 0:128])

    def along_rows_deep(which, value):
        return jnp.concatenate(
            [along_rows(which, value[0:256]), along_rows(which, value[128:384])], axis=0
        )

    def sides(turn):
        parts = []
        for group in range(4):
            from_left = left[turn, 32 * group : 32 * group + 32, :]
            from_right = right[turn, 32 * group : 32 * group + 32, :]
            parts.append(jnp.where(lane, from_right, from_left))
            parts.append(pltpu.roll(jnp.where(lane, from_left, from_right), 64, 1))
        return jnp.concatenate(parts, axis=0)

    def squares(difference):
        return jnp.sum(difference * difference, axis=0, keepdims=True)

    def norm_row(d):
        return pltpu.make_async_remote_copy(
            src_ref=partial,
            dst_ref=gather_rows.at[row],
            send_sem=norm_send.at[0],
            recv_sem=norm_recv.at[0],
            device_id=(lax.rem(row + d, rows), col),
            device_id_type=MESH,
        )

    def norm_col(d):
        return pltpu.make_async_remote_copy(
            src_ref=middle,
            dst_ref=gather_cols.at[col],
            send_sem=norm_send.at[1],
            recv_sem=norm_recv.at[1],
            device_id=(row, lax.rem(col + d, cols)),
            device_id_type=MESH,
        )

    def wait_all(buffer, count, semaphore):
        whole = buffer.at[pl.ds(0, count)]
        pltpu.make_async_copy(whole, whole, semaphore).wait()

    def start_norm_row(d, carry):
        norm_row(d).start()
        return carry

    def served(r, c):
        out = jnp.bool_(False)
        for e in early:
            out = out | ((r == e[0]) & (c == e[1]))
        return out

    def start_norm_col(d, carry):
        @pl.when(jnp.logical_not(served(row, lax.rem(col + d, cols))))
        def _():
            norm_col(d).start()

        return carry

    def direct(k):
        return pltpu.make_async_remote_copy(
            src_ref=partial,
            dst_ref=gather_all.at[row * cols + col],
            send_sem=norm_send.at[2 + k],
            recv_sem=norm_recv.at[2],
            device_id=early[k],
            device_id_type=MESH,
        )

    am_early = served(row, col)
    one_less = jnp.bool_(False)
    for e in early:
        one_less = one_less | ((row == e[0]) & (col != e[1]))

    def tell(level):
        for k, steps in enumerate(((1, 0), (0, 1))):
            if 1 << level < (rows, cols)[k] - 1:
                for sign in (-1, 1):
                    inside, device = near(tuple(sign * (1 << level) * s for s in steps))

                    @pl.when(inside)
                    def _():
                        pl.semaphore_signal(
                            known.at[level, k], inc=1, device_id=device, device_id_type=MESH
                        )

    def hear(level):
        for k, steps in enumerate(((1, 0), (0, 1))):
            if 1 << level < (rows, cols)[k] - 1:
                told = jnp.int32(0)
                for sign in (-1, 1):
                    inside, _ = near(tuple(sign * (1 << level) * s for s in steps))
                    told = told + inside.astype(jnp.int32)
                pl.semaphore_wait(known.at[level, k], told)

    load_start.wait()
    pack(0, jnp.where(lane_tall, field[0, 64:192, 0:128], field[0, 64:192, 384:512]))
    pl.semaphore_wait(barrier, expected)
    start(side_copies(0))
    start(row_copies(0, (0, 1, 2, 3)))
    tell(0)

    @pl.when(row == 0)
    def _():
        for k in (0, 2):
            field[k, 0:64, :] = jnp.zeros((64, 512), jnp.float32)
        ratio[0:128, :] = jnp.zeros((128, 512), jnp.float32)
        for buffer in (left, right):
            buffer[:, 0:32, :] = jnp.zeros((2, 32, 128), jnp.float32)
        for buffer in (deep_left, deep_right):
            buffer[0:128, :] = jnp.zeros((128, 128), jnp.float32)

    @pl.when(row == rows - 1)
    def _():
        for k in (0, 2):
            field[k, 192:256, :] = jnp.zeros((64, 512), jnp.float32)
        ratio[256:384, :] = jnp.zeros((128, 512), jnp.float32)
        for buffer in (left, right):
            buffer[:, 96:128, :] = jnp.zeros((2, 32, 128), jnp.float32)
        for buffer in (deep_left, deep_right):
            buffer[256:384, :] = jnp.zeros((128, 128), jnp.float32)

    @pl.when(col == 0)
    def _():
        left[...] = jnp.zeros((2, 128, 128), jnp.float32)
        deep_left[...] = jnp.zeros((384, 128), jnp.float32)

    @pl.when(col == cols - 1)
    def _():
        right[...] = jnp.zeros((2, 128, 128), jnp.float32)
        deep_right[...] = jnp.zeros((384, 128), jnp.float32)

    load_rows.wait()
    load_cols.wait()
    taps[...] = jnp.zeros((8, 256), jnp.float32)
    taps[0:1, 0:127] = taps_rows[...] / jnp.sum(taps_rows[...])
    taps[1:2, 0:127] = taps_cols[...] / jnp.sum(taps_cols[...])
    row_taps, col_taps = taps[0:1, :], taps[1:2, :]
    by_rows = (circulant(row_taps, 1, 128), circulant(row_taps, -127, 256)[:, :128].T)
    along = circulant(col_taps, -63, 256)
    by_cols = (along[:128].T, along[:, :128])
    for which in range(2):
        high, low = split(by_rows[which])
        row_mats[which, 0:128, :] = high
        row_mats[which, 128:256, :] = low
        high, low = split(by_cols[which])
        col_mats[which, :, 0:128] = high
        col_mats[which, :, 128:256] = low
    load_seen.wait()

    def at(b):
        return slice(128 * b, 128 * b + 128)

    def pair(value):
        return value[:, 0:128], value[:, 128:256]

    def outer_blocks(value):
        return jnp.concatenate([value[:, 0:128], value[:, 384:512]], axis=1)

    rounds = max(doublings(rows), doublings(cols))

    def spread(level):
        if level < rounds:
            hear(level)
            tell(level + 1)

    spread(0)

    blocks, outs = {}, {}
    arrive(row_copies(0, (1, 2)))
    blocks[1], blocks[2] = pair(along_rows(0, field[0, :, 128:384]))
    arrive(row_copies(0, (0, 3)))
    spread(1)
    blocks[0], blocks[3] = pair(along_rows(0, outer_blocks(field[0])))
    outs[1], outs[2] = along_cols(0, blocks, 1, 2)
    for b in (1, 2):
        ratio[128:256, at(b)] = seen[:, at(b)] / outs[b]
    start(deep_row_copies((1, 2)))
    outs[0], outs[3] = along_cols(0, blocks, 0, 3)
    seen_edge = jnp.where(lane_tall, seen[:, at(0)], seen[:, at(3)])
    edge = jnp.where(lane_tall, outs[0], outs[3])
    for b in (0, 3):
        ratio[128:256, at(b)] = seen[:, at(b)] / outs[b]
    inner_sum = squares(seen[:, at(1)] - outs[1]) + squares(seen[:, at(2)] - outs[2])
    inner_sum = inner_sum + squares(
        jnp.where(lane_tall, seen[:, at(3)] - outs[3], seen[:, at(0)] - outs[0])
    )
    arrive(side_copies(0))
    halo = sides(0)
    beside[...] = halo
    edge = edge + along_cols_edge(0, along_rows(0, halo))
    outer = seen_edge / edge
    ratio[128:256, at(0)] = jnp.where(lane_tall, outer, ratio[128:256, at(0)])
    ratio[128:256, at(3)] = jnp.where(lane_tall, ratio[128:256, at(3)], outer)
    start(deep_side_copies())
    start(deep_row_copies((0, 3)))
    first_norm = inner_sum + squares(seen_edge - edge)
    first_norm = first_norm + pltpu.roll(first_norm, 64, 1)
    spread(2)
    spread(3)

    blocks, outs = {}, {}
    arrive(deep_row_copies((1, 2)))
    blocks[1], blocks[2] = pair(along_rows_deep(1, ratio[:, 128:384]))
    arrive(deep_row_copies((0, 3)))
    blocks[0], blocks[3] = pair(along_rows_deep(1, outer_blocks(ratio)))
    outs[1], outs[2] = along_cols(1, blocks, 1, 2)
    for b in (1, 2):
        field[1, :, at(b)] = field[0, :, at(b)] * outs[b]
    outs[0], outs[3] = along_cols(1, blocks, 0, 3)
    again = {}
    again[1], again[2] = pair(along_rows(0, field[1, :, 128:384]))
    for level in range(4, rounds):
        spread(level)
    arrive(deep_side_copies())
    blocks[-1], blocks[4] = pair(
        along_rows_deep(1, jnp.concatenate([deep_left[...], deep_right[...]], axis=1))
    )
    edge = along_cols_edge(1, jnp.where(lane_deep, blocks[4], blocks[-1]))
    outs[-1], outs[4] = along_cols(1, blocks, -1, 4)
    field[1, :, at(0)] = field[0, :, at(0)] * jnp.where(lane_deep, outs[0] + edge, outs[0])
    field[1, :, at(3)] = field[0, :, at(3)] * jnp.where(lane_deep, outs[3], outs[3] + edge)
    halo = beside[...] * jnp.where(lane_deep, outs[4], outs[-1])

    again[0], again[3] = pair(along_rows(0, outer_blocks(field[1])))
    again[-1] = again[4] = along_rows(0, halo)
    outs = {}
    outs[0], outs[3] = along_cols(0, again, 0, 3)
    outs[1], outs[2] = along_cols(0, again, 1, 2)
    last_norm = sum(squares(seen[:, at(b)] - outs[b]) for b in range(4))
    last_norm = last_norm + pltpu.roll(last_norm, 64, 1)
    partial[...] = jnp.where(lane[0:1], first_norm, last_norm)
    gather_rows[row] = partial[...]
    for k, here in enumerate(is_early):

        @pl.when(here)
        def _():
            gather_all[row * cols + col] = partial[...]

        @pl.when(jnp.logical_not(here))
        def _():
            direct(k).start()

    lax.fori_loop(1, rows, start_norm_row, 0)
    for b in range(4):
        field[2, 64:192, at(b)] = seen[:, at(b)] / outs[b]
    pack(1, jnp.where(lane_tall, field[2, 64:192, at(0)], field[2, 64:192, at(3)]))
    start(side_copies(1))
    start(row_copies(1, (0, 1, 2, 3)))

    wait_all(gather_rows, rows - 1, norm_recv.at[0])
    total = gather_rows[0]
    for r in range(1, rows):
        total = total + gather_rows[r]
    middle[...] = total
    gather_cols[col] = total
    lax.fori_loop(1, cols, start_norm_col, 0)

    blocks, outs = {}, {}
    arrive(row_copies(1, (0, 1, 2, 3)))
    blocks[1], blocks[2] = pair(along_rows(1, field[2, :, 128:384]))
    blocks[0], blocks[3] = pair(along_rows(1, outer_blocks(field[2])))
    outs[1], outs[2] = along_cols(1, blocks, 1, 2)
    arrive(side_copies(1))
    blocks[-1] = blocks[4] = along_rows(1, sides(1))
    outs[0], outs[3] = along_cols(1, blocks, 0, 3)
    for b in range(4):
        result[:, at(b)] = field[1, 64:192, at(b)] * outs[b]

    store = pltpu.make_async_copy(result, out_ref, local.at[4])
    store.start()
    for turn in range(2):
        depart(side_copies(turn))
        depart(row_copies(turn, (0, 1, 2, 3)))
    depart(deep_side_copies())
    depart(deep_row_copies((0, 1, 2, 3)))
    wait_all(gather_rows, rows - 1, norm_send.at[0])
    place = lax.broadcasted_iota(jnp.int32, (1, 2), 1)

    def put_norms(total):
        first = jnp.sum(jnp.where(lane[0:1], total, 0.0), axis=1, keepdims=True)
        last = jnp.sum(jnp.where(lane[0:1], 0.0, total), axis=1, keepdims=True)
        norms_ref[...] = jnp.where(place == 0, first, last)

    @pl.when(am_early)
    def _():
        wait_all(gather_all, rows * cols - 1, norm_recv.at[2])
        total = None
        for c in range(cols):
            part = gather_all[c]
            for r in range(1, rows):
                part = part + gather_all[r * cols + c]
            total = part if total is None else total + part
        put_norms(total)

    @pl.when(jnp.logical_not(am_early))
    def _():
        wait_all(gather_cols, cols - 1, norm_recv.at[1])
        total = gather_cols[0]
        for c in range(1, cols):
            total = total + gather_cols[c]
        put_norms(total)

    @pl.when(one_less)
    def _():
        wait_all(gather_cols, cols - 2, norm_send.at[1])

    @pl.when(jnp.logical_not(one_less))
    def _():
        wait_all(gather_cols, cols - 1, norm_send.at[1])

    for k, here in enumerate(is_early):

        @pl.when(jnp.logical_not(here))
        def _():
            direct(k).wait_send()

    store.wait()


def finish(estimate, norms, out, out_norms, done):
    copies = (
        pltpu.make_async_copy(estimate, out, done.at[0]),
        pltpu.make_async_copy(norms, out_norms, done.at[1]),
    )
    for copy in copies:
        copy.start()
    for copy in copies:
        copy.wait()


def body(rows, cols, observed, start, psf_rows, psf_cols):
    f32, bf16 = jnp.float32, jnp.bfloat16
    estimate, norms = pl.pallas_call(
        functools.partial(kernel, rows, cols),
        out_shape=(
            jax.ShapeDtypeStruct((128, 512), f32),
            jax.ShapeDtypeStruct((1, 2), f32),
        ),
        in_specs=[
            pl.BlockSpec(memory_space=pltpu.HBM),
            pl.BlockSpec(memory_space=pltpu.HBM),
            pl.BlockSpec(memory_space=pltpu.HBM),
            pl.BlockSpec(memory_space=pltpu.HBM),
        ],
        out_specs=(
            pl.BlockSpec(memory_space=pl.ANY),
            pl.BlockSpec(memory_space=pltpu.VMEM),
        ),
        scratch_shapes=[
            pltpu.VMEM((3, 256, 512), f32),
            pltpu.VMEM((2, 128, 128), f32),
            pltpu.VMEM((2, 128, 128), f32),
            pltpu.VMEM((2, 64, 128), f32),
            pltpu.VMEM((2, 64, 128), f32),
            pltpu.VMEM((256, 128), f32),
            pltpu.VMEM((384, 512), f32),
            pltpu.VMEM((384, 128), f32),
            pltpu.VMEM((384, 128), f32),
            pltpu.VMEM((128, 512), f32),
            pltpu.VMEM((128, 512), f32),
            pltpu.VMEM((1, 127), f32),
            pltpu.VMEM((1, 127), f32),
            pltpu.VMEM((8, 256), f32),
            pltpu.VMEM((2, 256, 256), bf16),
            pltpu.VMEM((2, 256, 256), bf16),
            pltpu.VMEM((1, 128), f32),
            pltpu.VMEM((rows, 1, 128), f32),
            pltpu.VMEM((1, 128), f32),
            pltpu.VMEM((cols, 1, 128), f32),
            pltpu.VMEM((rows * cols, 1, 128), f32),
            pltpu.SemaphoreType.DMA((3, 6)),
            pltpu.SemaphoreType.DMA((3, 6)),
            pltpu.SemaphoreType.DMA((3, 2, 4)),
            pltpu.SemaphoreType.DMA((3, 2, 4)),
            pltpu.SemaphoreType.DMA((5,)),
            pltpu.SemaphoreType.DMA((2 + len(EARLY),)),
            pltpu.SemaphoreType.DMA((3,)),
            pltpu.SemaphoreType.REGULAR((max(doublings(rows), doublings(cols)), 2)),
        ],
        compiler_params=pltpu.CompilerParams(
            collective_id=0, has_side_effects=True, vmem_limit_bytes=54850 * 1024
        ),
        name="deconvolve",
    )(observed[0], start[0], psf_rows.reshape(1, 127), psf_cols.reshape(1, 127))
    estimate, norms = pl.pallas_call(
        finish,
        out_shape=(jax.ShapeDtypeStruct((128, 512), f32), jax.ShapeDtypeStruct((1, 2), f32)),
        in_specs=[pl.BlockSpec(memory_space=pl.ANY)] * 2,
        out_specs=[pl.BlockSpec(memory_space=pl.ANY)] * 2,
        scratch_shapes=[
            pltpu.SemaphoreType.DMA((2,)),
        ],
        compiler_params=pltpu.CompilerParams(vmem_limit_bytes=54850 * 1024),
        name="finish",
    )(estimate, norms)
    return estimate[None], norms.reshape(2)


def solution(mesh):
    in_specs = (P(None, "row", "col"), P(None, "row", "col"), P(), P())
    out_specs = (P(None, "row", "col"), P())
    step = functools.partial(body, mesh.shape["row"], mesh.shape["col"])
    return jax.shard_map(step, mesh=mesh, in_specs=in_specs, out_specs=out_specs, check_vma=False)
```
